256 devices in a mesh: radial: 64 (over z, y, core), chan: 4 (over x).
Axes of the slice: x: 4, y: 4, z: 8, core: 2. Of those that a mesh axis runs over, the one named last changes fastest.
Arguments:
- psi_outer: float32 [1024, 2, 49152], P('chan', None, 'radial'), may hold values from -6 to 6
- psi_inner: float32 [2, 24576], P(None, ('radial', 'chan')), may hold values from -6 to 6
- couplings: bfloat16 [2, 1024, 1024], P(None, None, 'chan'), as said below
- radial_parts: float32 [2, 49152], P(None, 'radial'), may hold values from 0.5 to 2
- labels: int32 [1024], replicated, may hold values from 0 to 47
- surface: bfloat16 [2, 1024, 24576], P(None, None, ('radial', 'chan')), may hold values from -0.25 to 0.25
- dipole_inner: bfloat16 [24576, 24576], P(('radial', 'chan')), may hold values from -1.5 to 1.5
- energies: float32 [24576], P(('radial', 'chan')), may hold values from -20 to 40
- block_sizes: int32 [32], replicated, may hold values from 384 to 768, as said below
- block_links: int32 [32, 32], replicated, may hold values from 0 to 1, as said below
- field: float32 [1], replicated, may hold values from 0.3 to 1
Outputs:
- outer_first: float32 [1024, 2, 49152], P('chan', None, 'radial')
- outer_second: float32 [1024, 2, 49152], P('chan', None, 'radial')
- inner_first: float32 [2, 24576], P(None, ('radial', 'chan'))
- inner_second: float32 [2, 24576], P(None, ('radial', 'chan'))
The draws below stay inside these ranges and needn't reach their ends.
Inputs may be any that keep to these rules, and one draw needn't show every extreme that they name: `couplings`: each of the two matrices is symmetric. `block_sizes`: one block holds all 768 functions. `block_links`: symmetric, one on the diagonal and between neighbouring blocks.
All inputs are finite; a program needn't handle non-finite values.
Results may differ from the reference program's by a relative error of at most 0.0025.
Values may be sent and summed in bfloat16 or wider, within the bound.
No kernel may reach another device: no remote copies, remote signals or barrier semaphores. Data moves between devices by JAX's collectives and lax.ppermute only.
A program may use at most 128 MiB of HBM per device.

```python
import math
import jax
import jax.numpy as jnp
from jax import lax

NCH = 1024
NB = 32
BCAP = 768
LMAX = 48
NR = 49152
NI = 24576
N_RADIAL = 64
N_CHAN = 4


def draw_psi_outer(key, part):
    key = jax.random.fold_in(key, 5)
    return jnp.clip(jax.random.normal(key, (NCH, 2, NR), jnp.float32), -6.0, 6.0)


def draw_couplings(key, part):
    key = jax.random.fold_in(key, 11)
    raw = jax.random.normal(key, (2, NCH, NCH), jnp.float32)
    factor = 1.5 / 1.4142135
    paired = (raw + jnp.swapaxes(raw, 1, 2)) * factor
    return paired.astype(jnp.bfloat16)


def draw_block_sizes(key, part):
    key = jax.random.fold_in(key, 23)
    first_key, second_key = jax.random.split(key)
    sizes_drawn = jax.random.randint(first_key, (NB,), BCAP // 2, BCAP + 1)
    chosen = jax.random.randint(second_key, (), 0, NB)
    return jnp.where(jnp.arange(NB) == chosen, BCAP, sizes_drawn).astype(jnp.int32)


def draw_block_links(key, part):
    key = jax.random.fold_in(key, 37)
    picks = (jax.random.randint(key, (NB, NB), 0, 20) < 3).astype(jnp.int32)
    row_ids = jnp.arange(NB)[:, None]
    col_ids = jnp.arange(NB)[None, :]
    symmetric = jnp.where(row_ids < col_ids, picks, picks.T)
    linked = jnp.where(jnp.abs(row_ids - col_ids) <= 1, 1, symmetric)
    return linked.astype(jnp.int32)


def set_ends(array, own_key, least, top_value):
    place = [jax.random.randint(jax.random.fold_in(own_key, axis), (), 0, length) for axis, length in enumerate(array.shape)]
    main_axis = array.shape.index(max(array.shape))
    next_to = place[:main_axis] + [(place[main_axis] + 1) % array.shape[main_axis]] + place[main_axis + 1:]
    return array.at[tuple(place)].set(least).at[tuple(next_to)].set(top_value)


def block_levels(stream_key, dims, cuts, least, high):
    def one(axis_at, parts):
        steps = jax.random.uniform(jax.random.fold_in(jax.random.fold_in(stream_key, 6), axis_at), (parts,), jnp.float32, least / len(cuts), high / len(cuts))
        return jnp.repeat(jnp.exp(steps), dims[axis_at] // parts).reshape((-1,) + (1,) * (len(dims) - axis_at - 1))

    factor_of = one(*cuts[0])
    for cut in cuts[1:]:
        factor_of = factor_of * one(*cut)
    return factor_of


def noise(rng, shape, scale, reach, pieces=(), held_as=jnp.bfloat16):
    drawn = jax.random.normal(rng, shape, jnp.float32) * scale
    if len(pieces) > 0:
        drawn = block_levels(rng, shape, pieces, -0.22, 0.18) * drawn
    return jnp.clip(drawn, min=-reach, max=reach).astype(held_as)


def setup_inputs(seed: int = 0) -> dict:
    key_of = jax.random.split(jax.random.key(seed), 12)
    return {
        "psi_outer": draw_psi_outer(jax.random.fold_in(key_of[11], 71), 0),
        "psi_inner": noise(key_of[1], (2, NI), 1.0, 6.0, ((1, 256),), jnp.float32),
        "couplings": draw_couplings(jax.random.fold_in(key_of[11], 71), 0),
        "radial_parts": jnp.clip(jnp.exp(math.log(2.0) - 1.3862944 * jax.random.uniform(key_of[3], (2, NR), jnp.float32) ** block_levels(key_of[3], (2, NR), ((1, 64),), -0.2, 0.2)), 0.5, 2.0),
        "labels": set_ends(jax.random.randint(key_of[4], (NCH,), 0, LMAX), jax.random.fold_in(key_of[4], 1), 0, LMAX - 1).astype(jnp.int32),
        "surface": noise(key_of[5], (2, NCH, NI), (3.0 / (NB * BCAP) ** 0.5), 0.25, ((2, 256),)),
        "dipole_inner": noise(key_of[6], (NI, NI), (1.0 / (NB * BCAP // (N_RADIAL * N_CHAN)) ** 0.5), 1.5, ((0, 256),)),
        "energies": jnp.clip(-20.0 + 60.0 * jax.random.uniform(key_of[7], (NI,), jnp.float32) ** block_levels(key_of[7], (NI,), ((0, 256),), -0.2, 0.2), -20.0, 40.0),
        "block_sizes": draw_block_sizes(jax.random.fold_in(key_of[11], 71), 0),
        "block_links": draw_block_links(jax.random.fold_in(key_of[11], 71), 0),
        "field": jnp.clip(jax.random.uniform(key_of[10], (1,), jnp.float32, 0.3, 1.0), 0.3, 1.0),
    }


step_width = 0.2
inner_radius = 20.0
time_step = 0.025


def reference(psi_outer, psi_inner, couplings, radial_parts, labels, surface, dipole_inner, energies, block_sizes, block_links, field):
    hi_prec = lax.Precision.HIGHEST
    index_all = jnp.arange(NB * BCAP, dtype=jnp.int32)
    block_of = index_all // BCAP
    active = ((index_all % BCAP) < block_sizes[block_of]).astype(jnp.float32)
    label_diff = labels[:, None] - labels[None, :]
    pair_zero = couplings[0].astype(jnp.float32) * (jnp.abs(label_diff) == 1).astype(jnp.float32)
    pair_one = couplings[1].astype(jnp.float32) * ((label_diff == 0) | (jnp.abs(label_diff) == 2)).astype(jnp.float32)
    surf_full = surface.astype(jnp.float32)
    positions = jnp.arange(NR, dtype=jnp.int32)
    radius = inner_radius + (positions + 1).astype(jnp.float32) * step_width
    label_float = labels.astype(jnp.float32)
    centrifugal = (label_float * (label_float + 1.0) / 2.0)[:, None, None] / (radius * radius)[None, None, :]
    dipole_row = jnp.tile(field[0] * radial_parts[0], 2)
    multipole_row = jnp.tile(radial_parts[1], 2)

    def hamiltonian(outer_state, inner_state):
        outer_low = lax.optimization_barrier(outer_state.astype(jnp.bfloat16)).astype(jnp.float32)
        inner_low = lax.optimization_barrier(inner_state.astype(jnp.bfloat16)).astype(jnp.float32)
        ghost_cells = jnp.einsum("kci,pi->cpk", surf_full, inner_low, precision=hi_prec)
        slope_value = (-3.0 * outer_state[:, :, 0] + 4.0 * outer_state[:, :, 1] - outer_state[:, :, 2]) / (2.0 * step_width)
        slope_low = lax.optimization_barrier(slope_value.astype(jnp.bfloat16)).astype(jnp.float32)
        padded = jnp.concatenate([ghost_cells, outer_state, jnp.zeros((NCH, 2, 2), jnp.float32)], axis=2)
        second_diff = (-padded[:, :, :-4] + 16.0 * padded[:, :, 1:-3] - 30.0 * padded[:, :, 2:-2]
                       + 16.0 * padded[:, :, 3:-1] - padded[:, :, 4:]) / (12.0 * step_width * step_width)
        flat_low = outer_low.reshape(NCH, 2 * NR)
        coupled = (jnp.dot(pair_zero, flat_low, precision=hi_prec) * dipole_row
                   + jnp.dot(pair_one, flat_low, precision=hi_prec) * multipole_row).reshape(NCH, 2, NR)
        outer_image = -0.5 * second_diff + centrifugal * outer_state + coupled

        def inner_block(block):
            row_block = lax.dynamic_slice_in_dim(dipole_inner, (block * BCAP).astype(jnp.int32), BCAP, 0).astype(jnp.float32)
            col_mask = block_links[block][block_of].astype(jnp.float32)
            return jnp.dot(row_block * col_mask[None, :], inner_low.T, precision=hi_prec)

        inner_product = lax.map(inner_block, jnp.arange(NB, dtype=jnp.int32)).reshape(NB * BCAP, 2).T
        bloch_term = 0.5 * jnp.einsum("ci,cp->pi", surf_full[1], slope_low, precision=hi_prec)
        inner_image = active[None, :] * (energies[None, :] * inner_state + field[0] * inner_product + bloch_term)
        return outer_image, inner_image

    inner_now = psi_inner * active[None, :]
    outer_image, inner_image = hamiltonian(psi_outer, inner_now)
    outer_first = time_step * jnp.stack([outer_image[:, 1], -outer_image[:, 0]], axis=1)
    inner_first = time_step * jnp.stack([inner_image[1], -inner_image[0]])
    outer_image, inner_image = hamiltonian(outer_first, inner_first)
    outer_second = 0.5 * time_step * jnp.stack([outer_image[:, 1], -outer_image[:, 0]], axis=1)
    inner_second = 0.5 * time_step * jnp.stack([inner_image[1], -inner_image[0]])
    return outer_first, outer_second, inner_first, inner_second
```

```python
import jax
import jax.numpy as jnp
from jax import lax
from jax.experimental import pallas as pl
from jax.experimental.pallas import tpu as pltpu
from jax.experimental.layout import Layout, with_layout_constraint
from jax.sharding import PartitionSpec as P

STEP = 0.2
INNER_RADIUS = 20.0
TAU = 0.025
LAP = 12.0 * STEP * STEP

CH = 256
ROWS = 12
NCHAN = 4
NDEV = 256
INNER = 96
HALF = 384
BCAP = 768

BF = jnp.bfloat16
F32 = jnp.float32
VMEM = pl.BlockSpec(memory_space=pltpu.VMEM)
SMEM = pl.BlockSpec(memory_space=pltpu.SMEM)


def sds(shape, dtype):
    return jax.ShapeDtypeStruct(shape, dtype)


def call(kernel, out_shape, specs, args, scratch=(), name=None, flops=0, nbytes=0, limit=60):
    return pl.pallas_call(
        kernel,
        out_shape=out_shape,
        in_specs=specs,
        out_specs=jax.tree.map(lambda _: VMEM, out_shape),
        scratch_shapes=list(scratch),
        name=name,
        cost_estimate=pl.CostEstimate(flops=flops, bytes_accessed=nbytes, transcendentals=0),
        compiler_params=pltpu.CompilerParams(vmem_limit_bytes=limit << 20),
    )(*args)


def lanes(shape):
    return lax.broadcasted_iota(jnp.int32, shape, len(shape) - 1)


def second_difference(x):
    width = x.shape[1]
    near = pltpu.roll(x, 1, 1) + pltpu.roll(x, width - 1, 1)
    far = pltpu.roll(x, 2, 1) + pltpu.roll(x, width - 2, 1)
    full = (16.0 * near - far - 30.0 * x) * (1.0 / LAP)
    return full[:, 128 : 128 + HALF]


def inverse_square(radial_index, h):
    pos = radial_index * 768 + h * HALF + lanes((1, HALF))
    radius = INNER_RADIUS + (pos + 1).astype(F32) * STEP
    return 1.0 / (radius * radius)


def half_square(lab):
    return lab * (lab + 1.0) * 0.5


def parity(lab):
    return lab.astype(jnp.int32) & 1


def halo_tile(right, left):
    rows = jnp.concatenate([right, jnp.zeros((96, CH), F32), left], axis=0)
    return rows.T


def edge_rows(tile0, tile5):
    lane = lanes((CH, 128))
    return jnp.where(lane < 5, tile0, jnp.where((lane == 14) | (lane == 15), pltpu.roll(tile5, 16, 1), 0.0))


def prepare_kernel(idx, u3, couplings, labels, m0, m1, m2, m3, e0, e1, e2, e3, edges, labcol, comb, comb_half):
    me = idx[0]
    core = idx[1] & 1
    lab_rows = jnp.broadcast_to(labels[...].astype(F32), (128, 1024))
    labcol[...] = lab_rows.T
    mine = labels[:, pl.ds(pl.multiple_of(me * CH, CH), CH)].astype(F32)
    for part in range(4):
        rows = pl.ds(part * 256, 256)
        gap = jnp.abs(labcol[rows, 0:1] - mine)
        zero = couplings[0, rows, :].astype(F32)
        one = couplings[1, rows, :].astype(F32)
        value = jnp.where(gap == 1.0, zero, jnp.where((gap == 0.0) | (gap == 2.0), one, 0.0))
        comb[rows, :] = value.astype(BF)
    comb_half[...] = comb[pl.ds(pl.multiple_of(core * 512, 512), 512), :]

    lane = lanes((CH, 128))
    picked = jnp.zeros((CH, 128), F32)
    for p in range(2):
        def tile(jb):
            return u3[pl.ds(2 * jb + p, CH, stride=ROWS), :]
        outer_edge = edge_rows(tile(0), tile(5))
        inner_edge = jnp.where(
            (lane == 16) | (lane == 17),
            pltpu.roll(tile(3), 16, 1),
            jnp.where((lane == 30) | (lane == 31), pltpu.roll(tile(2), 32, 1), 0.0),
        )
        both = outer_edge + inner_edge
        picked = picked + (both if p == 0 else pltpu.roll(both, 32, 1))
    edges[...] = picked.T[0:64, :]
    row8 = lax.broadcasted_iota(jnp.int32, (8, CH), 0)
    slab = jnp.where(row8 < 4, edges[0:8, :], pltpu.roll(edges[32:40, :], 4, 0))
    slab = jnp.concatenate([slab[:, 0:128], slab[:, 128:256]], axis=0).astype(BF)

    for s, (main, extra) in enumerate(zip((m0, m1, m2, m3), (e0, e1, e2, e3))):
        t = (me + s) & 3
        p = t >> 1
        h = t & 1
        for m in range(3):
            start = (3 * h + m) * 2 + p
            main[0:CH, 128 * m : 128 * m + 128] = u3[pl.ds(start, CH, stride=ROWS), :].astype(BF)
        base = pl.multiple_of(p * 32, 32)
        main[CH : CH + 16, 0:CH] = edges[pl.ds(base + 16, 16), :].astype(BF)
        main[CH : CH + 16, CH:HALF] = slab
        extra[...] = edges[pl.ds(base, 16), :].astype(BF)


def couple(comb, pair, labcol, radial_parts, field, t, h):
    rows = pl.ds(pl.multiple_of(t * CH, CH), CH)
    both = jnp.dot(comb[rows, :], pair[...], preferred_element_type=F32)
    even = parity(labcol[rows, 0:1]) == 0
    from_even, from_odd = both[:, :HALF], both[:, HALF:]
    cols = pl.ds(pl.multiple_of(h * HALF, 128), HALF)
    row0 = field[0] * radial_parts[0:1, cols]
    row1 = radial_parts[1:2, cols]
    return row1 * jnp.where(even, from_even, from_odd) + row0 * jnp.where(even, from_odd, from_even)


def first_couple_kernel(idx, field, m0, m1, m2, m3, e0, e1, e2, e3, comb_own, g1, g2, g3, q1, q2, q3, labcol,
                        radial_parts, c0, c1, c2, c3, comb, pair2, pair1):
    me = idx[0]
    rad = idx[1]
    core = rad & 1
    p = me >> 1
    h = me & 1
    mains = (m0, m1, m2, m3)
    extras = (e0, e1, e2, e3)
    comb[:, 0:CH] = comb_own[...]
    ours = pl.ds(pl.multiple_of(core * 512, 512), 512)
    others = pl.ds(pl.multiple_of((1 - core) * 512, 512), 512)
    for s, (got, swapped) in enumerate(zip((g1, g2, g3), (q1, q2, q3)), 1):
        comb[ours, s * CH : (s + 1) * CH] = got[...]
        comb[others, s * CH : (s + 1) * CH] = swapped[...]
    for s in range(4):
        src = (me - s) & 3
        odd = parity(labcol[pl.ds(pl.multiple_of(src * CH, CH), CH), 0:1]).astype(F32)
        u = mains[s][0:CH, :].astype(F32)
        pair1[s * CH : (s + 1) * CH, 0:HALF] = (u * (1.0 - odd)).astype(BF)
        pair1[s * CH : (s + 1) * CH, HALF:] = (u * odd).astype(BF)
    inv = inverse_square(rad, h)
    scale = jnp.where(p == 1, TAU, -TAU)
    for target, out in enumerate((c0, c1, c2, c3)):
        t = (me + target) & 3
        coupled = couple(comb, pair1, labcol, radial_parts, field, t, h)
        out[...] = coupled.astype(BF)
        s = (4 - target) % 4
        inside = mains[s][CH : CH + 16, 0:CH].astype(F32)
        outside = extras[s][...].astype(F32)
        halo = halo_tile(jnp.where(h == 0, inside, outside), jnp.where(h == 0, outside, inside))
        u = mains[s][0:CH, :].astype(F32)
        lap = second_difference(jnp.concatenate([halo, u, halo], axis=1))
        lab = labcol[pl.ds(pl.multiple_of(t * CH, CH), CH), 0:1]
        value = scale * (coupled - 0.5 * lap + half_square(lab) * inv * u)
        value = value.astype(BF).astype(F32)
        odd = parity(lab).astype(F32)
        pair2[s * CH : (s + 1) * CH, 0:HALF] = (value * (1.0 - odd)).astype(BF)
        pair2[s * CH : (s + 1) * CH, HALF:] = (value * odd).astype(BF)


def second_couple_kernel(idx, field, comb, pair2, labcol, radial_parts, c0, c1, c2, c3):
    me = idx[0]
    for target, out in enumerate((c0, c1, c2, c3)):
        t = (me + target) & 3
        out[...] = couple(comb, pair2, labcol, radial_parts, field, t, me & 1).astype(BF)


def taylor(scale, flip, idx, u3, low, high, cs, labcol, out3, padded):
    me = idx[0]
    rad = idx[1]
    for p in range(2):
        halo = halo_tile(high[p * 32 : p * 32 + 16, :], low[p * 32 : p * 32 + 16, :])
        padded[p, :, 0:128] = halo
        padded[p, :, 896:1024] = halo
        for jb in range(6):
            padded[p, :, 128 * (jb + 1) : 128 * (jb + 2)] = u3[pl.ds(2 * jb + p, CH, stride=ROWS), :]
    lab = labcol[pl.ds(pl.multiple_of(me * CH, CH), CH), 0:1]
    centrifugal = half_square(lab)
    for s in range(4):
        t = (me - s) & 3
        p = (t >> 1) ^ flip
        h = t & 1
        x = padded[p, :, pl.ds(pl.multiple_of(h * HALF, 128), 640)]
        lap = second_difference(x)
        u = x[:, 128 : 128 + HALF]
        value = cs[s][...].astype(F32) - 0.5 * lap + centrifugal * inverse_square(rad, h) * u
        value = jnp.where(p == 1, scale, -scale) * value
        for m in range(3):
            out3[pl.ds((3 * h + m) * 2 + 1 - p, CH, stride=ROWS), :] = value[:, 128 * m : 128 * m + 128]


def first_term_kernel(idx, u3, low, high, c0, c1, c2, c3, labcol, out3, edges, padded):
    taylor(TAU, 0, idx, u3, low, high, (c0, c1, c2, c3), labcol, out3, padded)
    picked = jnp.zeros((CH, 128), F32)
    for p in range(2):
        tile = edge_rows(out3[pl.ds(p, CH, stride=ROWS), :], out3[pl.ds(10 + p, CH, stride=ROWS), :])
        picked = picked + (tile if p == 0 else pltpu.roll(tile, 32, 1))
    edges[...] = picked.T[0:64, :]


def second_term_kernel(idx, u3, low, high, c0, c1, c2, c3, labcol, out3, padded):
    taylor(0.5 * TAU, 1, idx, u3, low, high, (c0, c1, c2, c3), labcol, out3, padded)


def split_couple(rows, comb, labels, me):
    odd = parity(labels[...]).astype(F32)
    from_even = jnp.dot((rows * (1.0 - odd)).astype(BF), comb[...], preferred_element_type=F32)
    from_odd = jnp.dot((rows * odd).astype(BF), comb[...], preferred_element_type=F32)
    mine_odd = parity(labels[:, pl.ds(pl.multiple_of(me * CH, CH), CH)]) == 1
    same = jnp.where(mine_odd, from_odd, from_even)
    other = jnp.where(mine_odd, from_even, from_odd)
    return same, other


def boundary_kernel(idx, field, m0, m1, m2, m3, comb, edges, labels, radial_parts, out, rows):
    me = idx[0]
    for s, main in enumerate((m0, m1, m2, m3)):
        src = (me - s) & 3
        block = main[CH : CH + 16, CH:HALF].astype(F32)
        at = pl.multiple_of(src * CH, CH)
        rows[:, pl.ds(at, 128)] = block[0:8]
        rows[:, pl.ds(at + 128, 128)] = block[8:16]
    same, other = split_couple(rows[...], comb, labels, me)
    mine = labels[:, pl.ds(pl.multiple_of(me * CH, CH), CH)].astype(F32)
    image = []
    for p in range(2):
        w = [edges[p * 32 + j : p * 32 + j + 1, :] for j in range(5)]
        laps = (
            16.0 * w[1] - w[2] - 30.0 * w[0],
            16.0 * (w[0] + w[2]) - 30.0 * w[1] - w[3],
            16.0 * (w[1] + w[3]) - 30.0 * w[2] - w[0] - w[4],
        )
        terms = []
        for j in range(3):
            radius = INNER_RADIUS + (j + 1) * STEP
            r = p * 4 + j
            coupled = (field[0] * radial_parts[0:1, j : j + 1] * other[r : r + 1, :]
                       + radial_parts[1:2, j : j + 1] * same[r : r + 1, :])
            terms.append(-0.5 / LAP * laps[j] + half_square(mine) * (1.0 / (radius * radius)) * w[j] + coupled)
        image.append((4.0 * terms[1] - 3.0 * terms[0] - terms[2]) * (1.0 / (2.0 * STEP)))
    out[0:1, :] = TAU * image[1]
    out[1:2, :] = -TAU * image[0]


def ghost_image(g):
    image = [(-0.5 / LAP * (16.0 * g[p][1] - g[p][0]), 0.5 / LAP * g[p][1]) for p in range(2)]
    return [[TAU * image[1][j] for j in range(2)], [-TAU * image[0][j] for j in range(2)]]


def ghost_rows(ghosts, q):
    return [[ghosts[pl.ds((p * 2 + k) * 4 + q, 1), :] for k in range(2)] for p in range(2)]


def fix_kernel(idx, field, first_in, second_in, ghosts, b0, b1, b2, b3, comb, labels, radial_parts, first, second,
               rows):
    me = idx[0]
    on = jnp.where(idx[1] == 0, 1.0, 0.0)
    rows[...] = jnp.zeros((8, 1024), F32)
    for q in range(4):
        image = ghost_image(ghost_rows(ghosts, q))
        for p in range(2):
            for j in range(2):
                low = image[p][j].astype(BF).astype(F32)
                rows[p * 4 + j : p * 4 + j + 1, q * CH : (q + 1) * CH] = low
    same, other = split_couple(rows[...], comb, labels, me)
    mine = labels[:, pl.ds(pl.multiple_of(me * CH, CH), CH)].astype(F32)
    added = ghost_image(ghost_rows(ghosts, me))
    later = ((b0, b1), (b2, b3))
    images = []
    for p in range(2):
        g0, g1 = [jnp.concatenate([later[p][k][0:1, :], later[p][k][1:2, :]], axis=1) for k in range(2)]
        f0, f1 = added[p]
        laps = (16.0 * (f1 + g1) - 30.0 * f0 - g0, 16.0 * f0 - 30.0 * f1 - g1, 16.0 * f1 - f0, -f1)
        terms = [-0.5 / LAP * lap for lap in laps]
        for j in range(2):
            radius = INNER_RADIUS + (j + 1) * STEP
            r = p * 4 + j
            terms[j] = (terms[j] + half_square(mine) * (1.0 / (radius * radius)) * added[p][j]
                        + field[0] * radial_parts[0:1, j : j + 1] * other[r : r + 1, :]
                        + radial_parts[1:2, j : j + 1] * same[r : r + 1, :])
        images.append(terms)

    def columns(values):
        row = lax.broadcasted_iota(jnp.int32, (128, CH), 0)
        spread = jnp.zeros((128, CH), F32)
        for j, value in enumerate(values):
            spread = jnp.where(row == j, jnp.broadcast_to(value, (128, CH)), spread)
        return (spread * on).T

    for p in range(2):
        first[:, p, :] = first_in[:, p, :] + columns(added[p])
        sign = 0.5 * TAU if p == 0 else -0.5 * TAU
        second[:, p, :] = second_in[:, p, :] + columns([sign * term for term in images[1 - p]])


def active_row(idx, sizes):
    dev = idx[2]
    place = (dev & 7) * INNER + lanes((1, INNER))
    return (place < sizes[dev >> 3]).astype(F32)


def pad_row(row):
    return jnp.concatenate([row, jnp.zeros((row.shape[0], 128 - row.shape[1]), F32)], axis=1)


def low_rows(v):
    return jnp.concatenate([v, jnp.zeros((6, INNER), F32)], axis=0).astype(BF)


def fill(message, rows):
    tile = jnp.concatenate(rows, axis=0)
    message[...] = jnp.broadcast_to(tile[None], (NDEV, 8, 128)).reshape(NDEV * 8, 128)


def inner_prepare_kernel(idx, sizes, psi, edges, surface, out, now, message, table):
    v = psi[...] * active_row(idx, sizes)
    now[...] = v
    low = low_rows(v)
    slopes = []
    for p in range(2):
        w = [edges[p * 32 + j : p * 32 + j + 1, :] for j in range(3)]
        slope = (4.0 * w[1] - 3.0 * w[0] - w[2]) * (1.0 / (2.0 * STEP))
        slopes += [slope[:, 0:128], slope[:, 128:256]]
    lows = pad_row(v)
    fill(message, slopes + [lows[0:1], lows[1:2], jnp.zeros((2, 128), F32)])
    table[...] = jnp.zeros((128, CH), F32)
    for k in range(2):
        part = jnp.dot(low, surface[k], preferred_element_type=F32)
        for p in range(2):
            for q in range(4):
                at = (p * 2 + k) * 4 + q
                table[at : at + 1, :] = part[p : p + 1, q * CH : (q + 1) * CH]
    mine = table[...].T
    high = mine.astype(BF).astype(F32)
    message[pl.ds(6, NDEV, stride=8), :] = high + pltpu.roll(mine - high, 16, 1)
    out[...] = message[...].reshape(NDEV, 8, 128).astype(BF)


def apply_inner(idx, field, sizes, links, energies, got, dipole, surface, v, slope_row, table):
    block = idx[2] >> 3
    lane = lanes((64, 128))
    for p in range(2):
        x = [got[pl.ds(4 + p + 8 * q, 64, stride=32), :] for q in range(4)]
        table[p, 0] = jnp.where(lane < 96, x[0], pltpu.roll(x[1], 96, 1))
        table[p, 1] = jnp.where(lane < 64, pltpu.roll(x[1], 96, 1), pltpu.roll(x[2], 64, 1))
        table[p, 2] = jnp.where(lane < 32, pltpu.roll(x[2], 64, 1), pltpu.roll(x[3], 32, 1))

    def step(g, totals):
        link = links[block, g >> 1].astype(F32)
        totals = list(totals)
        for m in range(3):
            tile = dipole[:, pl.ds(pl.multiple_of(g * 384 + m * 128, 128), 128)].astype(F32)
            for p in range(2):
                totals[p] = totals[p] + tile * (table[p, m, pl.ds(g, 1), :] * link)
        return tuple(totals)

    zero = jnp.zeros((INNER, 128), F32)
    products = lax.fori_loop(0, 64, step, (zero, zero), unroll=2)
    rows = []
    for p in range(2):
        bloch = zero
        for block128 in range(8):
            tile = surface[1, :, block128 * 128 : block128 * 128 + 128].astype(F32)
            bloch = bloch + tile * slope_row(p, block128)
        total = field[0] * products[p] + 0.5 * bloch
        total = jnp.concatenate([total, jnp.zeros((32, 128), F32)], axis=0)
        rows.append(jnp.sum(total.T, axis=0, keepdims=True)[:, 0:INNER])
    image = energies[...] * v + jnp.concatenate(rows, axis=0)
    return active_row(idx, sizes) * image


def turned(scale, image):
    return jnp.concatenate([scale * image[1:2], -scale * image[0:1]], axis=0)


def inner_first_kernel(idx, field, sizes, links, received, dipole, surface, now, energies, slope, out, term,
                       got, table, message):
    got[...] = received[...].astype(F32).reshape(NDEV * 8, 128)

    def slope_row(p, block128):
        src, half = block128 // 2, block128 % 2
        at = 8 * src + 2 * p + half
        return got[at : at + 1, :]

    image = apply_inner(idx, field, sizes, links, energies, got, dipole, surface, now[...], slope_row, table)
    value = turned(TAU, image)
    term[...] = value
    low = low_rows(value)
    sums = jnp.sum(got[pl.ds(6, NDEV, stride=8), :], axis=0, keepdims=True)
    sums = sums + pltpu.roll(sums, 112, 1)
    lane = lanes((1, 128))
    sums = jnp.where(lane < 16, sums, 0.0)
    high = sums.astype(BF).astype(F32)
    lows = pad_row(value)
    slopes = []
    for p in range(2):
        slopes += [slope[p : p + 1, 0:128], slope[p : p + 1, 128:256]]
    fill(message, slopes + [lows[0:1] + pltpu.roll(high, 96, 1), lows[1:2] + pltpu.roll(sums - high, 96, 1),
                            jnp.zeros((2, 128), F32)])
    for k in range(2):
        part = jnp.dot(low, surface[k], preferred_element_type=F32)
        for p in range(2):
            for c in range(4):
                dest = (p * 2 + k) * 4 + c
                for half in range(2):
                    at = dest * 8 + 6 + half
                    lo = c * CH + half * 128
                    message[at : at + 1, :] = part[p : p + 1, lo : lo + 128]
    out[...] = message[...].reshape(NDEV, 8, 128).astype(BF)


def inner_second_kernel(idx, field, sizes, links, received, dipole, surface, first, energies, term, ghosts,
                        got, table, slopes):
    got[...] = received[...].astype(F32).reshape(NDEV * 8, 128)
    lane = lanes((NDEV, 128))
    pairs = jnp.where(lane < 112, got[pl.ds(4, NDEV, stride=8), :] + got[pl.ds(5, NDEV, stride=8), :], 0.0)
    ghosts[...] = pltpu.roll(pairs, 32, 1).T[0:16, :]
    for q in range(4):
        image = ghost_image(ghost_rows(ghosts, q))
        for p in range(2):
            extra = (4.0 * image[p][1] - 3.0 * image[p][0]) * (1.0 / (2.0 * STEP))
            for half in range(2):
                at = 8 * q + 2 * p + half
                total = got[at : at + 1, :] + extra[:, half * 128 : half * 128 + 128]
                row = p * 8 + q * 2 + half
                slopes[row : row + 1, :] = total.astype(BF).astype(F32)

    def slope_row(p, block128):
        return slopes[p * 8 + block128 : p * 8 + block128 + 1, :]

    image = apply_inner(idx, field, sizes, links, energies, got, dipole, surface, first[...], slope_row, table)
    term[...] = turned(0.5 * TAU, image)


def body(psi_outer, psi_inner, couplings, radial_parts, labels, surface, dipole_inner, energies, block_sizes,
         block_links, field):
    me = lax.axis_index("chan")
    rad = lax.axis_index("radial")
    idx = jnp.stack([me, rad, rad * NCHAN + me, jnp.zeros_like(me)]).astype(jnp.int32)
    everyone = ("radial", "chan")
    count = 64

    def chan_shift(x, s):
        return lax.ppermute(x, "chan", [(i, (i + s) % NCHAN) for i in range(NCHAN)])

    def core_swap(x):
        return lax.ppermute(x, "radial", [(i, i ^ 1) for i in range(count)])

    def edge_shift(x, s):
        pairs = []
        for r in range(count):
            for c in range(NCHAN):
                t = (c + s) % NCHAN
                to = r + 1 if t % 2 == 0 else r - 1
                if 0 <= to < count:
                    pairs.append((r * NCHAN + c, to * NCHAN + t))
        return lax.ppermute(x, everyone, pairs)

    def sector_shift(x):
        low = lax.ppermute(x, "radial", [(i, i + 1) for i in range(count - 1)])
        high = lax.ppermute(x, "radial", [(i + 1, i) for i in range(count - 1)])
        return low, high

    def exchange(x):
        return lax.all_to_all(x, everyone, 0, 0, tiled=True)

    tiles_first = Layout(major_to_minor=(0, 2, 1, 3))

    def flat(x):
        x = with_layout_constraint(x.reshape(CH, 2, 6, 128), tiles_first)
        return x.transpose(0, 2, 1, 3).reshape(CH * ROWS, 128)

    def unflat(x):
        x = with_layout_constraint(x.reshape(CH, 6, 2, 128).transpose(0, 2, 1, 3), tiles_first)
        return x.reshape(CH, 2, 768)

    u3 = flat(psi_outer)
    lab = labels.reshape(1, 1024)
    surf = jnp.swapaxes(surface, 1, 2)
    energy = energies.reshape(1, INNER)
    main_shape = sds((CH + 16, HALF), BF)
    edge_shape = sds((16, CH), BF)
    piece = sds((CH, HALF), BF)

    prepared = call(
        prepare_kernel,
        (main_shape,) * 4 + (edge_shape,) * 4
        + (sds((64, CH), F32), sds((1024, 128), F32), sds((1024, CH), BF), sds((512, CH), BF)),
        [SMEM, VMEM, VMEM, VMEM], (idx, u3, couplings, lab), name="prepare", nbytes=6 << 20)
    mains, extras = prepared[0:4], prepared[4:8]
    edges, labcol, comb_own, comb_half = prepared[8:]

    got_main = [mains[0]] + [chan_shift(mains[s], s) for s in (1, 3, 2)]
    got_main = [got_main[0], got_main[1], got_main[3], got_main[2]]
    got_comb = {s: chan_shift(comb_half, s) for s in (1, 3, 2)}
    got_extra = [edge_shift(extras[s], s) for s in range(4)]
    low, high = sector_shift(edges)
    swapped = {s: core_swap(got_comb[s]) for s in (1, 3, 2)}

    message1, now = call(
        inner_prepare_kernel, (sds((NDEV, 8, 128), BF), sds((2, INNER), F32)),
        [SMEM, SMEM, VMEM, VMEM, VMEM], (idx, block_sizes, psi_inner, edges, surf),
        [pltpu.VMEM((NDEV * 8, 128), F32), pltpu.VMEM((128, CH), F32)], name="inner_prepare", nbytes=2 << 20)
    received1 = exchange(message1)

    slope = call(
        boundary_kernel, sds((2, CH), F32), [SMEM, SMEM] + [VMEM] * 8,
        (idx, field, *got_main, comb_own, edges, lab, radial_parts),
        [pltpu.VMEM((8, 1024), F32)], name="boundary", nbytes=2 << 20)

    coupled = call(
        first_couple_kernel, (piece,) * 4 + (sds((1024, 1024), BF), sds((1024, 2 * HALF), BF)),
        [SMEM, SMEM] + [VMEM] * 17,
        (idx, field, *got_main, *got_extra, comb_own, got_comb[1], got_comb[2], got_comb[3], swapped[1], swapped[2],
         swapped[3], labcol, radial_parts),
        [pltpu.VMEM((1024, 2 * HALF), BF)], name="first_couple", flops=2 * 1024 * 1024 * 768, nbytes=10 << 20)
    first_pieces, comb_all, pair2 = coupled[0:4], coupled[4], coupled[5]
    back1 = [first_pieces[0]] + [chan_shift(first_pieces[s], s) for s in (1, 2, 3)]

    second_pieces = call(
        second_couple_kernel, (piece,) * 4, [SMEM, SMEM] + [VMEM] * 4,
        (idx, field, comb_all, pair2, labcol, radial_parts), name="second_couple",
        flops=2 * 1024 * 1024 * 768, nbytes=6 << 20)
    back2 = [second_pieces[0]] + [chan_shift(second_pieces[s], s) for s in (1, 2, 3)]

    first3, first_edges = call(
        first_term_kernel, (sds((CH * ROWS, 128), F32), sds((64, CH), F32)), [SMEM] + [VMEM] * 8,
        (idx, u3, low, high, *back1, labcol), [pltpu.VMEM((2, CH, 1024), F32)], name="first_term", nbytes=6 << 20)
    low2, high2 = sector_shift(first_edges)

    message2, inner_first = call(
        inner_first_kernel, (sds((NDEV, 8, 128), BF), sds((2, INNER), F32)),
        [SMEM] * 4 + [VMEM] * 6,
        (idx, field, block_sizes, block_links, received1, dipole_inner, surf, now, energy, slope),
        [pltpu.VMEM((NDEV * 8, 128), F32), pltpu.VMEM((2, 3, 64, 128), F32), pltpu.VMEM((NDEV * 8, 128), F32)],
        name="inner_first", nbytes=8 << 20)
    received2 = exchange(message2)

    second3 = call(
        second_term_kernel, sds((CH * ROWS, 128), F32), [SMEM] + [VMEM] * 8,
        (idx, first3, low2, high2, *back2, labcol), [pltpu.VMEM((2, CH, 1024), F32)], name="second_term",
        nbytes=6 << 20)

    sums = jnp.sum(received2[:, 6:8, :].astype(F32), axis=0)
    later = [sums] + [lax.ppermute(sums, "radial", [(j, 0)]) for j in (1, 2, 3)]

    inner_second, ghosts = call(
        inner_second_kernel, (sds((2, INNER), F32), sds((16, CH), F32)), [SMEM] * 4 + [VMEM] * 5,
        (idx, field, block_sizes, block_links, received2, dipole_inner, surf, inner_first, energy),
        [pltpu.VMEM((NDEV * 8, 128), F32), pltpu.VMEM((2, 3, 64, 128), F32), pltpu.VMEM((16, 128), F32)],
        name="inner_second", nbytes=8 << 20)

    tile = pl.BlockSpec((CH, 2, 128), lambda i: (0, 0, 0))
    outer_shape = sds((CH, 2, 768), F32)
    outer_first, outer_second = pl.pallas_call(
        fix_kernel, out_shape=(outer_shape, outer_shape), grid=(1,),
        in_specs=[SMEM, SMEM, tile, tile] + [VMEM] * 8, out_specs=(tile, tile),
        scratch_shapes=[pltpu.VMEM((8, 1024), F32)], input_output_aliases={2: 0, 3: 1}, name="fix",
        cost_estimate=pl.CostEstimate(flops=0, bytes_accessed=2 << 20, transcendentals=0),
        compiler_params=pltpu.CompilerParams(vmem_limit_bytes=60 << 20),
    )(idx, field, unflat(first3), unflat(second3), ghosts, *later, comb_own, lab, radial_parts)
    return outer_first, outer_second, inner_first, inner_second


def solution(mesh):
    in_specs = (
        P("chan", None, "radial"),
        P(None, ("radial", "chan")),
        P(None, None, "chan"),
        P(None, "radial"),
        P(),
        P(None, None, ("radial", "chan")),
        P(("radial", "chan"), None),
        P(("radial", "chan")),
        P(),
        P(),
        P(),
    )
    out_specs = (
        P("chan", None, "radial"),
        P("chan", None, "radial"),
        P(None, ("radial", "chan")),
        P(None, ("radial", "chan")),
    )
    return jax.shard_map(body, mesh=mesh, in_specs=in_specs, out_specs=out_specs, check_vma=False)
```

```python
import jax
import jax.numpy as jnp
from jax import lax
from jax.experimental import pallas as pl
from jax.experimental.pallas import tpu as pltpu
from jax.experimental.layout import Layout, with_layout_constraint
from jax.sharding import PartitionSpec as P

STEP = 0.2
INNER_RADIUS = 20.0
TAU = 0.025
LAP = 12.0 * STEP * STEP

CH = 256
ROWS = 12
NCHAN = 4
NDEV = 256
INNER = 96
HALF = 384
PART = CH + 32
PIECE = 3 * PART
BCAP = 768
CHUNK = 32
BOUNDARY_FLOPS = 10**10

BF = jnp.bfloat16
F32 = jnp.float32
VMEM = pl.BlockSpec(memory_space=pltpu.VMEM)
SMEM = pl.BlockSpec(memory_space=pltpu.SMEM)


def sds(shape, dtype):
    return jax.ShapeDtypeStruct(shape, dtype)


def call(kernel, out_shape, specs, args, scratch=(), name=None, flops=0, limit=60):
    return pl.pallas_call(
        kernel,
        out_shape=out_shape,
        in_specs=specs,
        out_specs=jax.tree.map(lambda _: VMEM, out_shape),
        scratch_shapes=list(scratch),
        name=name,
        cost_estimate=pl.CostEstimate(flops=flops, bytes_accessed=0, transcendentals=0),
        compiler_params=pltpu.CompilerParams(vmem_limit_bytes=limit << 20),
    )(*args)


def lanes(shape):
    return lax.broadcasted_iota(jnp.int32, shape, len(shape) - 1)


def second_difference(x):
    width = x.shape[1]
    near = pltpu.roll(x, 1, 1) + pltpu.roll(x, width - 1, 1)
    far = pltpu.roll(x, 2, 1) + pltpu.roll(x, width - 2, 1)
    return (16.0 * near - far - 30.0 * x) * (1.0 / LAP)


def inverse_square(start, width):
    pos = start + lanes((1, width))
    radius = INNER_RADIUS + (pos + 1).astype(F32) * STEP
    return 1.0 / (radius * radius)


def half_square(lab):
    return lab * (lab + 1.0) * 0.5


def parity(lab):
    return lab.astype(jnp.int32) & 1


def halo_tile(right, left):
    rows = jnp.concatenate([right, jnp.zeros((96, CH), F32), left], axis=0)
    return rows.T


def edge_rows(tile0, tile5):
    lane = lanes((CH, 128))
    return jnp.where(lane < 5, tile0, jnp.where((lane >= 12) & (lane < 16), pltpu.roll(tile5, 16, 1), 0.0))


def prepare_kernel(idx, u3, couplings, labels, radial_parts, m0, m1, m2, m3, edges, labcol, comb):
    me = idx[0]
    core = idx[1] & 1
    lab_rows = jnp.broadcast_to(labels[...].astype(F32), (128, 1024))
    labcol[...] = lab_rows.T
    mine = labels[:, pl.ds(pl.multiple_of(me * CH, CH), CH)].astype(F32)
    for part in range(4):
        rows = pl.ds(part * 256, 256)
        gap = jnp.abs(labcol[rows, 0:1] - mine)
        zero = couplings[0, rows, :].astype(F32)
        one = couplings[1, rows, :].astype(F32)
        value = jnp.where(gap == 1.0, zero, jnp.where((gap == 0.0) | (gap == 2.0), one, 0.0))
        comb[rows, :] = value.astype(BF)
    half = comb[pl.ds(pl.multiple_of(core * 512, 512), 512), :]
    for pack in (m1, m2, m3):
        pack[PIECE : PIECE + 512, :] = half[:, 0:128]
        pack[PIECE + 512 : PIECE + 1024, :] = half[:, 128:256]

    lane = lanes((CH, 128))
    picked = jnp.zeros((CH, 128), F32)
    for p in range(2):
        def tile(jb):
            return u3[pl.ds(2 * jb + p, CH, stride=ROWS), :]
        outer_edge = edge_rows(tile(0), tile(5))
        inner_edge = jnp.where(
            (lane == 16) | (lane == 17),
            pltpu.roll(tile(3), 16, 1),
            jnp.where((lane == 30) | (lane == 31), pltpu.roll(tile(2), 32, 1), 0.0),
        )
        both = outer_edge + inner_edge
        picked = picked + (both if p == 0 else pltpu.roll(both, 32, 1))
    edges[0:64, :] = picked.T[0:64, :]
    edges[64:66, :] = radial_parts[:, 0:256]
    edges[66:68, :] = radial_parts[:, 512:768]
    edges[68:72, :] = jnp.zeros((4, CH), F32)
    row8 = lax.broadcasted_iota(jnp.int32, (8, CH), 0)
    slab = jnp.where(row8 < 4, edges[0:8, :], pltpu.roll(edges[32:40, :], 4, 0))
    slab = jnp.concatenate([slab[:, 0:128], slab[:, 128:256]], axis=0).astype(BF)

    for s, main in enumerate((m0, m1, m2, m3)):
        t = (me + s) & 3
        p = t >> 1
        h = t & 1
        base = pl.multiple_of(p * 32, 32)
        inside = edges[pl.ds(base + 16, 16), :].astype(BF)
        own = edges[pl.ds(base, 16), :].astype(BF)
        tails = (inside[:, 0:128], inside[:, 128:256], slab)
        ends = (own[:, 0:128], own[:, 128:256], slab)
        for m in range(3):
            start = (3 * h + m) * 2 + p
            main[PART * m : PART * m + CH, :] = u3[pl.ds(start, CH, stride=ROWS), :].astype(BF)
            main[PART * m + CH : PART * m + CH + 16, :] = tails[m]
            main[PART * m + CH + 16 : PART * (m + 1), :] = ends[m]


def couple_kernel(idx, field, m0, m1, m2, m3, beyond, comb_own, q1, q2, q3, low, high, labcol, radial_parts,
                  c0, c1, c2, c3, comb, pair1, pair2, halos, both):
    me = idx[0]
    rad = idx[1]
    core = rad & 1
    p = me >> 1
    h = me & 1
    mains = (m0, m1, m2, m3)
    comb[:, 0:CH] = comb_own[...]
    ours = pl.ds(pl.multiple_of(core * 512, 512), 512)
    others = pl.ds(pl.multiple_of((1 - core) * 512, 512), 512)
    for s, (got, swapped) in enumerate(zip((m1, m2, m3), (q1, q2, q3)), 1):
        for half in range(2):
            at = s * CH + half * 128
            src = PIECE + 512 * half
            comb[ours, at : at + 128] = got[src : src + 512, :]
            comb[others, at : at + 128] = swapped[src : src + 512, :]
    wide = HALF + 128
    for s in range(4):
        src = (me - s) & 3
        odd = parity(labcol[pl.ds(pl.multiple_of(src * CH, CH), CH), 0:1]).astype(F32)
        rows = slice(s * CH, (s + 1) * CH)
        main = mains[s]
        inside = jnp.concatenate([main[CH : CH + 16, :], main[PART + CH : PART + CH + 16, :]], axis=1).astype(F32)
        outside = beyond[:, pl.ds(pl.multiple_of(src * CH, CH), CH)].astype(F32)
        halo = halo_tile(jnp.where(h == 0, inside, outside), jnp.where(h == 0, outside, inside))
        halos[s] = halo
        even16 = (1.0 - odd).astype(BF)
        odd16 = odd.astype(BF)
        tiles = [main[PART * m : PART * m + CH, :] for m in range(3)] + [halo.astype(BF)]
        for m, tile in enumerate(tiles):
            pair1[rows, 128 * m : 128 * m + 128] = tile * even16
            pair1[rows, wide + 128 * m : wide + 128 * m + 128] = tile * odd16
    for n in range(4):
        cols = slice(n * 256, n * 256 + 256)
        both[:, cols] = jnp.dot(comb[...], pair1[:, cols], preferred_element_type=F32)
    inv = inverse_square(rad * 768 + h * HALF, HALF)
    scale = jnp.where(p == 1, TAU, -TAU)
    cols = pl.ds(pl.multiple_of(h * HALF, 128), HALF)
    near = lanes((1, 128)) < 64
    row0 = jnp.concatenate(
        [radial_parts[0:1, cols], jnp.where(near, high[64:65, 0:128], low[66:67, 128:256])], axis=1) * field[0]
    row1 = jnp.concatenate(
        [radial_parts[1:2, cols], jnp.where(near, high[65:66, 0:128], low[67:68, 128:256])], axis=1)
    outs = (c0, c1, c2, c3)
    for target, out in enumerate(outs):
        t = (me + target) & 3
        s = (4 - target) % 4

        def first_rows(i, _, t=t, s=s, out=out):
            here = pl.multiple_of(i * CHUNK, CHUNK)
            rows = pl.ds(pl.multiple_of(t * CH + i * CHUNK, CHUNK), CHUNK)
            lab = labcol[rows, 0:1]
            even = parity(lab) == 0
            a, b = both[rows, 0:wide], both[rows, wide : 2 * wide]
            coupled = row1 * jnp.where(even, a, b) + row0 * jnp.where(even, b, a)
            out[pl.ds(here, CHUNK), 0:wide] = coupled.astype(BF)
            u = [mains[s][pl.ds(PART * m + here, CHUNK), :].astype(F32) for m in range(3)]
            halo = halos[s, pl.ds(here, CHUNK), :]
            x = jnp.concatenate([halo] + u + [halo], axis=1)
            lap = second_difference(x)[:, 128 : 128 + HALF]
            value = scale * (coupled[:, 0:HALF] - 0.5 * lap + half_square(lab) * inv * x[:, 128 : 128 + HALF])
            spot = pl.ds(pl.multiple_of(s * CH + here, CHUNK), CHUNK)
            pair2[spot, 0:HALF] = jnp.where(even, value, 0.0).astype(BF)
            pair2[spot, HALF:] = jnp.where(even, 0.0, value).astype(BF)
            return 0

        lax.fori_loop(0, CH // CHUNK, first_rows, 0)
    for n in range(3):
        cols = slice(n * 256, n * 256 + 256)
        both[:, cols] = jnp.dot(comb[...], pair2[:, cols], preferred_element_type=F32)
    for target, out in enumerate(outs):
        t = (me + target) & 3

        def second_rows(i, _, t=t, out=out):
            here = pl.multiple_of(i * CHUNK, CHUNK)
            rows = pl.ds(pl.multiple_of(t * CH + i * CHUNK, CHUNK), CHUNK)
            even = parity(labcol[rows, 0:1]) == 0
            a, b = both[rows, 0:HALF], both[rows, HALF : 2 * HALF]
            coupled = row1[:, 0:HALF] * jnp.where(even, a, b) + row0[:, 0:HALF] * jnp.where(even, b, a)
            out[pl.ds(here, CHUNK), wide:] = coupled.astype(BF)
            return 0

        lax.fori_loop(0, CH // CHUNK, second_rows, 0)


def terms_kernel(idx, u3, low, high, c0, c1, c2, c3, labcol, first3, second3, padded, turned_first):
    me = idx[0]
    rad = idx[1]
    cs = (c0, c1, c2, c3)
    for p in range(2):
        halo = halo_tile(high[p * 32 : p * 32 + 16, :], low[p * 32 : p * 32 + 16, :])
        padded[p, :, 0:128] = halo
        padded[p, :, 896:1024] = halo
        for jb in range(6):
            padded[p, :, 128 * (jb + 1) : 128 * (jb + 2)] = u3[pl.ds(2 * jb + p, CH, stride=ROWS), :]
    wide = HALF + 128
    for s in range(4):
        t = (me - s) & 3
        p = t >> 1
        h = t & 1
        scale = jnp.where(p == 1, TAU, -TAU)
        inv = inverse_square(rad * 768 + h * HALF, HALF)
        side_inv = inverse_square(rad * 768 - 128 + h * 896, 128)
        side_scale = jnp.where(((rad == 0) & (h == 0)) | ((rad == 63) & (h == 1)), 0.0, scale)

        def first_rows(i, _, p=p, h=h, scale=scale, inv=inv, side_inv=side_inv, side_scale=side_scale, c=cs[s]):
            here = pl.multiple_of(i * CHUNK, CHUNK)
            rows = pl.ds(here, CHUNK)
            centrifugal = half_square(labcol[pl.ds(pl.multiple_of(me * CH + here, CHUNK), CHUNK), 0:1])
            x = padded[p, rows, pl.ds(pl.multiple_of(h * HALF, 128), 640)]
            lap = second_difference(x)
            coupled = c[rows, 0:wide].astype(F32)
            value = scale * (coupled[:, 0:HALF] - 0.5 * lap[:, 128 : 128 + HALF]
                             + centrifugal * inv * x[:, 128 : 128 + HALF])
            turned_first[1 - p, rows, pl.ds(pl.multiple_of(h * HALF + 128, 128), HALF)] = value
            for m in range(3):
                at = (3 * h + m) * 2 + 1 - p + here * ROWS
                first3[pl.ds(at, CHUNK, stride=ROWS), :] = value[:, 128 * m : 128 * m + 128]
            side = jnp.where(h == 0, x[:, 0:128], x[:, 512:640])
            side_lap = jnp.where(h == 0, lap[:, 0:128], lap[:, 512:640])
            value = side_scale * (coupled[:, HALF:] - 0.5 * side_lap + centrifugal * side_inv * side)
            turned_first[1 - p, rows, pl.ds(pl.multiple_of(h * 896, 128), 128)] = value
            return 0

        lax.fori_loop(0, CH // CHUNK, first_rows, 0)
    for s in range(4):
        t = (me - s) & 3
        p = 1 - (t >> 1)
        h = t & 1
        scale = jnp.where(p == 1, 0.5 * TAU, -0.5 * TAU)
        inv = inverse_square(rad * 768 + h * HALF, HALF)

        def second_rows(i, _, p=p, h=h, scale=scale, inv=inv, c=cs[s]):
            here = pl.multiple_of(i * CHUNK, CHUNK)
            rows = pl.ds(here, CHUNK)
            centrifugal = half_square(labcol[pl.ds(pl.multiple_of(me * CH + here, CHUNK), CHUNK), 0:1])
            x = turned_first[p, rows, pl.ds(pl.multiple_of(h * HALF, 128), 640)]
            lap = second_difference(x)[:, 128 : 128 + HALF]
            value = scale * (c[rows, wide:].astype(F32) - 0.5 * lap + centrifugal * inv * x[:, 128 : 128 + HALF])
            for m in range(3):
                at = (3 * h + m) * 2 + 1 - p + here * ROWS
                second3[pl.ds(at, CHUNK, stride=ROWS), :] = value[:, 128 * m : 128 * m + 128]
            return 0

        lax.fori_loop(0, CH // CHUNK, second_rows, 0)


def split_couple(rows, comb, labels, me):
    odd = parity(labels[...]).astype(F32)
    from_even = jnp.dot((rows * (1.0 - odd)).astype(BF), comb[...], preferred_element_type=F32)
    from_odd = jnp.dot((rows * odd).astype(BF), comb[...], preferred_element_type=F32)
    mine_odd = parity(labels[:, pl.ds(pl.multiple_of(me * CH, CH), CH)]) == 1
    same = jnp.where(mine_odd, from_odd, from_even)
    other = jnp.where(mine_odd, from_even, from_odd)
    return same, other


def boundary_kernel(idx, field, m0, m1, m2, m3, comb, edges, labels, radial_parts, out, own, rows):
    me = idx[0]
    for s, main in enumerate((m0, m1, m2, m3)):
        src = (me - s) & 3
        block = main[2 * PART + CH : 2 * PART + CH + 16, :].astype(F32)
        at = pl.multiple_of(src * CH, CH)
        rows[:, pl.ds(at, 128)] = block[0:8]
        rows[:, pl.ds(at + 128, 128)] = block[8:16]
        for half in range(2):
            own[:, pl.ds(at + 128 * half, 128)] = main[PART * half + CH + 16 : PART * half + CH + 32, :]
    same, other = split_couple(rows[...], comb, labels, me)
    mine = labels[:, pl.ds(pl.multiple_of(me * CH, CH), CH)].astype(F32)
    image = []
    for p in range(2):
        w = [edges[p * 32 + j : p * 32 + j + 1, :] for j in range(5)]
        laps = (
            16.0 * w[1] - w[2] - 30.0 * w[0],
            16.0 * (w[0] + w[2]) - 30.0 * w[1] - w[3],
            16.0 * (w[1] + w[3]) - 30.0 * w[2] - w[0] - w[4],
        )
        terms = []
        for j in range(3):
            radius = INNER_RADIUS + (j + 1) * STEP
            r = p * 4 + j
            coupled = (field[0] * radial_parts[0:1, j : j + 1] * other[r : r + 1, :]
                       + radial_parts[1:2, j : j + 1] * same[r : r + 1, :])
            terms.append(-0.5 / LAP * laps[j] + half_square(mine) * (1.0 / (radius * radius)) * w[j] + coupled)
        image.append((4.0 * terms[1] - 3.0 * terms[0] - terms[2]) * (1.0 / (2.0 * STEP)))
    out[0:1, :] = TAU * image[1]
    out[1:2, :] = -TAU * image[0]


def ghost_image(g):
    image = [(-0.5 / LAP * (16.0 * g[p][1] - g[p][0]), 0.5 / LAP * g[p][1]) for p in range(2)]
    return [[TAU * image[1][j] for j in range(2)], [-TAU * image[0][j] for j in range(2)]]


def ghost_rows(ghosts, q):
    return [[ghosts[pl.ds((p * 2 + k) * 4 + q, 1), :] for k in range(2)] for p in range(2)]


def fix_kernel(idx, field, first_in, second_in, ghosts, b0, b1, b2, b3, comb, labels, radial_parts, first, second,
               rows):
    me = idx[0]
    on = jnp.where(idx[1] == 0, 1.0, 0.0)
    rows[...] = jnp.zeros((8, 1024), F32)
    for q in range(4):
        image = ghost_image(ghost_rows(ghosts, q))
        for p in range(2):
            for j in range(2):
                low = image[p][j].astype(BF).astype(F32)
                rows[p * 4 + j : p * 4 + j + 1, q * CH : (q + 1) * CH] = low
    same, other = split_couple(rows[...], comb, labels, me)
    mine = labels[:, pl.ds(pl.multiple_of(me * CH, CH), CH)].astype(F32)
    added = ghost_image(ghost_rows(ghosts, me))
    later = ((b0, b1), (b2, b3))
    images = []
    for p in range(2):
        g0, g1 = [jnp.concatenate([later[p][k][0:1, :], later[p][k][1:2, :]], axis=1) for k in range(2)]
        f0, f1 = added[p]
        laps = (16.0 * (f1 + g1) - 30.0 * f0 - g0, 16.0 * f0 - 30.0 * f1 - g1, 16.0 * f1 - f0, -f1)
        terms = [-0.5 / LAP * lap for lap in laps]
        for j in range(2):
            radius = INNER_RADIUS + (j + 1) * STEP
            r = p * 4 + j
            terms[j] = (terms[j] + half_square(mine) * (1.0 / (radius * radius)) * added[p][j]
                        + field[0] * radial_parts[0:1, j : j + 1] * other[r : r + 1, :]
                        + radial_parts[1:2, j : j + 1] * same[r : r + 1, :])
        images.append(terms)

    def columns(values):
        row = lax.broadcasted_iota(jnp.int32, (128, CH), 0)
        spread = jnp.zeros((128, CH), F32)
        for j, value in enumerate(values):
            spread = jnp.where(row == j, jnp.broadcast_to(value, (128, CH)), spread)
        return (spread * on).T

    for p in range(2):
        first[:, p, :] = first_in[:, p, :] + columns(added[p])
        sign = 0.5 * TAU if p == 0 else -0.5 * TAU
        second[:, p, :] = second_in[:, p, :] + columns([sign * term for term in images[1 - p]])


def active_row(idx, sizes):
    dev = idx[2]
    place = (dev & 7) * INNER + lanes((1, INNER))
    return (place < sizes[dev >> 3]).astype(F32)


def pad_row(row):
    return jnp.concatenate([row, jnp.zeros((row.shape[0], 128 - row.shape[1]), F32)], axis=1)


def low_rows(v):
    return jnp.concatenate([v, jnp.zeros((6, INNER), F32)], axis=0).astype(BF)


def fill(message, rows):
    tile = jnp.concatenate(rows, axis=0)
    message[...] = jnp.broadcast_to(tile[None], (NDEV, 8, 128)).reshape(NDEV * 8, 128)


def inner_prepare_kernel(idx, sizes, psi, edges, surface, out, now, message, table):
    v = psi[...] * active_row(idx, sizes)
    now[...] = v
    low = low_rows(v)
    slopes = []
    for p in range(2):
        w = [edges[p * 32 + j : p * 32 + j + 1, :] for j in range(3)]
        slope = (4.0 * w[1] - 3.0 * w[0] - w[2]) * (1.0 / (2.0 * STEP))
        slopes += [slope[:, 0:128], slope[:, 128:256]]
    lows = pad_row(v)
    fill(message, slopes + [lows[0:1], lows[1:2], jnp.zeros((2, 128), F32)])
    table[...] = jnp.zeros((128, CH), F32)
    for k in range(2):
        part = jnp.dot(low, surface[k], preferred_element_type=F32)
        for p in range(2):
            for q in range(4):
                at = (p * 2 + k) * 4 + q
                table[at : at + 1, :] = part[p : p + 1, q * CH : (q + 1) * CH]
    mine = table[...].T
    high = mine.astype(BF).astype(F32)
    message[pl.ds(6, NDEV, stride=8), :] = high + pltpu.roll(mine - high, 16, 1)
    out[...] = message[...].reshape(NDEV, 8, 128).astype(BF)


def apply_inner(idx, field, sizes, links, energies, got, dipole, surface, v, slope_row, table):
    block = idx[2] >> 3
    lane = lanes((64, 128))
    for p in range(2):
        x = [got[pl.ds(4 + p + 8 * q, 64, stride=32), :] for q in range(4)]
        table[p, 0] = jnp.where(lane < 96, x[0], pltpu.roll(x[1], 96, 1))
        table[p, 1] = jnp.where(lane < 64, pltpu.roll(x[1], 96, 1), pltpu.roll(x[2], 64, 1))
        table[p, 2] = jnp.where(lane < 32, pltpu.roll(x[2], 64, 1), pltpu.roll(x[3], 32, 1))

    def step(g, totals):
        link = links[block, g >> 1].astype(F32)
        totals = list(totals)
        for m in range(3):
            tile = dipole[:, pl.ds(pl.multiple_of(g * 384 + m * 128, 128), 128)].astype(F32)
            for p in range(2):
                totals[p] = totals[p] + tile * (table[p, m, pl.ds(g, 1), :] * link)
        return tuple(totals)

    zero = jnp.zeros((INNER, 128), F32)
    products = lax.fori_loop(0, 64, step, (zero, zero), unroll=2)
    rows = []
    for p in range(2):
        bloch = zero
        for block128 in range(8):
            tile = surface[1, :, block128 * 128 : block128 * 128 + 128].astype(F32)
            bloch = bloch + tile * slope_row(p, block128)
        total = field[0] * products[p] + 0.5 * bloch
        total = jnp.concatenate([total, jnp.zeros((32, 128), F32)], axis=0)
        rows.append(jnp.sum(total.T, axis=0, keepdims=True)[:, 0:INNER])
    image = energies[...] * v + jnp.concatenate(rows, axis=0)
    return active_row(idx, sizes) * image


def turned(scale, image):
    return jnp.concatenate([scale * image[1:2], -scale * image[0:1]], axis=0)


def inner_first_kernel(idx, field, sizes, links, received, dipole, surface, now, energies, slope, out, term,
                       got, table, message):
    got[...] = received[...].astype(F32).reshape(NDEV * 8, 128)

    def slope_row(p, block128):
        src, half = block128 // 2, block128 % 2
        at = 8 * src + 2 * p + half
        return got[at : at + 1, :]

    image = apply_inner(idx, field, sizes, links, energies, got, dipole, surface, now[...], slope_row, table)
    value = turned(TAU, image)
    term[...] = value
    low = low_rows(value)
    sums = jnp.sum(got[pl.ds(6, NDEV, stride=8), :], axis=0, keepdims=True)
    sums = sums + pltpu.roll(sums, 112, 1)
    lane = lanes((1, 128))
    sums = jnp.where(lane < 16, sums, 0.0)
    high = sums.astype(BF).astype(F32)
    lows = pad_row(value)
    slopes = []
    for p in range(2):
        slopes += [slope[p : p + 1, 0:128], slope[p : p + 1, 128:256]]
    fill(message, slopes + [lows[0:1] + pltpu.roll(high, 96, 1), lows[1:2] + pltpu.roll(sums - high, 96, 1),
                            jnp.zeros((2, 128), F32)])
    for k in range(2):
        part = jnp.dot(low, surface[k], preferred_element_type=F32)
        for p in range(2):
            for c in range(4):
                dest = (p * 2 + k) * 4 + c
                for half in range(2):
                    at = dest * 8 + 6 + half
                    lo = c * CH + half * 128
                    message[at : at + 1, :] = part[p : p + 1, lo : lo + 128]
    out[...] = message[...].reshape(NDEV, 8, 128).astype(BF)


def inner_second_kernel(idx, field, sizes, links, received, dipole, surface, first, energies, term, ghosts,
                        got, table, slopes):
    got[...] = received[...].astype(F32).reshape(NDEV * 8, 128)
    lane = lanes((NDEV, 128))
    pairs = jnp.where(lane < 112, got[pl.ds(4, NDEV, stride=8), :] + got[pl.ds(5, NDEV, stride=8), :], 0.0)
    ghosts[...] = pltpu.roll(pairs, 32, 1).T[0:16, :]
    for q in range(4):
        image = ghost_image(ghost_rows(ghosts, q))
        for p in range(2):
            extra = (4.0 * image[p][1] - 3.0 * image[p][0]) * (1.0 / (2.0 * STEP))
            for half in range(2):
                at = 8 * q + 2 * p + half
                total = got[at : at + 1, :] + extra[:, half * 128 : half * 128 + 128]
                row = p * 8 + q * 2 + half
                slopes[row : row + 1, :] = total.astype(BF).astype(F32)

    def slope_row(p, block128):
        return slopes[p * 8 + block128 : p * 8 + block128 + 1, :]

    image = apply_inner(idx, field, sizes, links, energies, got, dipole, surface, first[...], slope_row, table)
    term[...] = turned(0.5 * TAU, image)


def body(psi_outer, psi_inner, couplings, radial_parts, labels, surface, dipole_inner, energies, block_sizes,
         block_links, field):
    me = lax.axis_index("chan")
    rad = lax.axis_index("radial")
    idx = jnp.stack([me, rad, rad * NCHAN + me, jnp.zeros_like(me)]).astype(jnp.int32)
    everyone = ("radial", "chan")
    count = 64

    def chan_shift(x, s):
        return lax.ppermute(x, "chan", [(i, (i + s) % NCHAN) for i in range(NCHAN)])

    def core_swap(x):
        return lax.ppermute(x, "radial", [(i, i ^ 1) for i in range(count)])

    def edge_shift(x):
        pairs = []
        for r in range(count):
            for c in range(NCHAN):
                to, t = (r - 1, c + 1) if c % 2 == 0 else (r + 1, c - 1)
                if 0 <= to < count:
                    pairs.append((r * NCHAN + c, to * NCHAN + t))
        return lax.ppermute(x, everyone, pairs)

    def sector_shift(x):
        low = lax.ppermute(x, "radial", [(i, i + 1) for i in range(count - 1)])
        high = lax.ppermute(x, "radial", [(i + 1, i) for i in range(count - 1)])
        return low, high

    def exchange(x):
        return lax.all_to_all(x, everyone, 0, 0, tiled=True)

    tiles_first = Layout(major_to_minor=(0, 2, 1, 3))

    def flat(x):
        x = with_layout_constraint(x.reshape(CH, 2, 6, 128), tiles_first)
        return x.transpose(0, 2, 1, 3).reshape(CH * ROWS, 128)

    def unflat(x):
        x = with_layout_constraint(x.reshape(CH, 6, 2, 128).transpose(0, 2, 1, 3), tiles_first)
        return x.reshape(CH, 2, 768)

    u3 = flat(psi_outer)
    lab = labels.reshape(1, 1024)
    surf = jnp.swapaxes(surface, 1, 2)
    energy = energies.reshape(1, INNER)
    pack_shape = sds((PIECE + 1024, 128), BF)
    piece = sds((CH, 2 * HALF + 128), BF)

    prepared = call(
        prepare_kernel,
        (sds((PIECE, 128), BF),) + (pack_shape,) * 3
        + (sds((72, CH), F32), sds((1024, 128), F32), sds((1024, CH), BF)),
        [SMEM, VMEM, VMEM, VMEM, VMEM], (idx, u3, couplings, lab, radial_parts), name="prepare")
    packs = prepared[0:4]
    edges, labcol, comb_own = prepared[4:]

    got = {s: chan_shift(packs[s], s) for s in (2, 1, 3)}
    low, high = sector_shift(edges)
    mains = (packs[0], got[1], got[2], got[3])
    mains, low, high = lax.optimization_barrier((mains, low, high))

    message1, now = call(
        inner_prepare_kernel, (sds((NDEV, 8, 128), BF), sds((2, INNER), F32)),
        [SMEM, SMEM, VMEM, VMEM, VMEM], (idx, block_sizes, psi_inner, edges, surf),
        [pltpu.VMEM((NDEV * 8, 128), F32), pltpu.VMEM((128, CH), F32)], name="inner_prepare")
    received1 = exchange(message1)

    slope, own = call(
        boundary_kernel, (sds((2, CH), F32), sds((16, 1024), BF)), [SMEM, SMEM] + [VMEM] * 8,
        (idx, field, *mains, comb_own, edges, lab, radial_parts),
        [pltpu.VMEM((8, 1024), F32)], name="boundary", flops=BOUNDARY_FLOPS)
    swapped = {s: core_swap(mains[s]) for s in (1, 3, 2)}
    beyond = edge_shift(own)
    received1, swapped, beyond = lax.optimization_barrier((received1, swapped, beyond))

    pieces = call(
        couple_kernel, (piece,) * 4, [SMEM, SMEM] + [VMEM] * 13,
        (idx, field, *mains, beyond, comb_own, swapped[1], swapped[2], swapped[3], low, high, labcol,
         radial_parts),
        [pltpu.VMEM((1024, 1024), BF), pltpu.VMEM((1024, 2 * HALF + 256), BF), pltpu.VMEM((1024, 2 * HALF), BF),
         pltpu.VMEM((4, CH, 128), F32), pltpu.VMEM((1024, 1024), F32)], name="couple")
    back = [pieces[0]] + [chan_shift(pieces[s], s) for s in (1, 2, 3)]

    first3, second3 = call(
        terms_kernel, (sds((CH * ROWS, 128), F32),) * 2, [SMEM] + [VMEM] * 8,
        (idx, u3, low, high, *back, labcol), [pltpu.VMEM((2, CH, 1024), F32)] * 2, name="terms")

    message2, inner_first = call(
        inner_first_kernel, (sds((NDEV, 8, 128), BF), sds((2, INNER), F32)),
        [SMEM] * 4 + [VMEM] * 6,
        (idx, field, block_sizes, block_links, received1, dipole_inner, surf, now, energy, slope),
        [pltpu.VMEM((NDEV * 8, 128), F32), pltpu.VMEM((2, 3, 64, 128), F32), pltpu.VMEM((NDEV * 8, 128), F32)],
        name="inner_first")
    received2 = exchange(message2)

    sums = jnp.sum(received2[:, 6:8, :].astype(F32), axis=0)
    later = [sums] + [lax.ppermute(sums, "radial", [(j, 0)]) for j in (1, 2, 3)]

    inner_second, ghosts = call(
        inner_second_kernel, (sds((2, INNER), F32), sds((16, CH), F32)), [SMEM] * 4 + [VMEM] * 5,
        (idx, field, block_sizes, block_links, received2, dipole_inner, surf, inner_first, energy),
        [pltpu.VMEM((NDEV * 8, 128), F32), pltpu.VMEM((2, 3, 64, 128), F32), pltpu.VMEM((16, 128), F32)],
        name="inner_second")

    tile = pl.BlockSpec((CH, 2, 128), lambda i: (0, 0, 0))
    outer_shape = sds((CH, 2, 768), F32)
    outer_first, outer_second = pl.pallas_call(
        fix_kernel, out_shape=(outer_shape, outer_shape), grid=(1,),
        in_specs=[SMEM, SMEM, tile, tile] + [VMEM] * 8, out_specs=(tile, tile),
        scratch_shapes=[pltpu.VMEM((8, 1024), F32)], input_output_aliases={2: 0, 3: 1}, name="fix",
        cost_estimate=pl.CostEstimate(flops=0, bytes_accessed=0, transcendentals=0),
        compiler_params=pltpu.CompilerParams(vmem_limit_bytes=60 << 20),
    )(idx, field, unflat(first3), unflat(second3), ghosts, *later, comb_own, lab, radial_parts)
    return outer_first, outer_second, inner_first, inner_second


def solution(mesh):
    in_specs = (
        P("chan", None, "radial"),
        P(None, ("radial", "chan")),
        P(None, None, "chan"),
        P(None, "radial"),
        P(),
        P(None, None, ("radial", "chan")),
        P(("radial", "chan"), None),
        P(("radial", "chan")),
        P(),
        P(),
        P(),
    )
    out_specs = (
        P("chan", None, "radial"),
        P("chan", None, "radial"),
        P(None, ("radial", "chan")),
        P(None, ("radial", "chan")),
    )
    return jax.shard_map(body, mesh=mesh, in_specs=in_specs, out_specs=out_specs, check_vma=False)
```

```python
import jax
import jax.numpy as jnp
from jax import lax
from jax.experimental import pallas as pl
from jax.experimental.pallas import tpu as pltpu
from jax.experimental.layout import Layout, with_layout_constraint
from jax.sharding import PartitionSpec as P

STEP = 0.2
INNER_RADIUS = 20.0
TAU = 0.025
LAP = 12.0 * STEP * STEP

CH = 256
ROWS = 12
NCHAN = 4
NDEV = 256
INNER = 96
HALF = 384
PART = CH + 32
PIECE = 3 * PART
BCAP = 768
BOUNDARY_FLOPS = 10**10

BF = jnp.bfloat16
F32 = jnp.float32
VMEM = pl.BlockSpec(memory_space=pltpu.VMEM)
SMEM = pl.BlockSpec(memory_space=pltpu.SMEM)
ANY = pl.BlockSpec(memory_space=pl.ANY)


def sds(shape, dtype):
    return jax.ShapeDtypeStruct(shape, dtype)


def call(kernel, out_shape, specs, args, scratch=(), name=None, flops=0, limit=60):
    return pl.pallas_call(
        kernel,
        out_shape=out_shape,
        in_specs=specs,
        out_specs=jax.tree.map(lambda _: VMEM, out_shape),
        scratch_shapes=list(scratch),
        name=name,
        cost_estimate=pl.CostEstimate(flops=flops, bytes_accessed=0, transcendentals=0),
        compiler_params=pltpu.CompilerParams(vmem_limit_bytes=limit << 20),
    )(*args)


def lanes(shape):
    return lax.broadcasted_iota(jnp.int32, shape, len(shape) - 1)


def stencil(depth, width):
    gap = jnp.abs(lax.broadcasted_iota(jnp.int32, (depth, width), 0) - lanes((depth, width)) - 128)
    weight = jnp.where(gap == 0, -30.0, jnp.where(gap == 1, 16.0, jnp.where(gap == 2, -1.0, 0.0)))
    return weight.astype(BF)


def matmul(a, b):
    return jnp.dot(a, b, preferred_element_type=F32)


def inverse_square(start, width):
    pos = start + lanes((1, width))
    radius = INNER_RADIUS + (pos + 1).astype(F32) * STEP
    return 1.0 / (radius * radius)


def half_square(lab):
    return lab * (lab + 1.0) * 0.5


def parity(lab):
    return lab.astype(jnp.int32) & 1


def halo_tile(right, left):
    rows = jnp.concatenate([right, jnp.zeros((96, CH), F32), left], axis=0)
    return rows.T


def edge_rows(tile0, tile5):
    lane = lanes((CH, 128))
    return jnp.where(lane < 5, tile0, jnp.where((lane >= 12) & (lane < 16), pltpu.roll(tile5, 16, 1), 0.0))


def prepare_kernel(idx, u3, couplings, labels, radial_parts, m0, m1, m2, m3, edges, labcol, comb):
    me = idx[0]
    core = idx[1] & 1
    lab_rows = jnp.broadcast_to(labels[...].astype(F32), (128, 1024))
    labcol[...] = lab_rows.T
    mine = labels[:, pl.ds(pl.multiple_of(me * CH, CH), CH)].astype(F32)
    for part in range(4):
        rows = pl.ds(part * 256, 256)
        gap = jnp.abs(labcol[rows, 0:1] - mine)
        zero = couplings[0, rows, :].astype(F32)
        one = couplings[1, rows, :].astype(F32)
        value = jnp.where(gap == 1.0, zero, jnp.where((gap == 0.0) | (gap == 2.0), one, 0.0))
        comb[rows, :] = value.astype(BF)
    half = comb[pl.ds(pl.multiple_of(core * 512, 512), 512), :]
    for pack in (m1, m2, m3):
        pack[PIECE : PIECE + 512, :] = half[:, 0:128]
        pack[PIECE + 512 : PIECE + 1024, :] = half[:, 128:256]

    lane = lanes((CH, 128))
    picked = jnp.zeros((CH, 128), F32)
    for p in range(2):
        def tile(jb):
            return u3[pl.ds(2 * jb + p, CH, stride=ROWS), :]
        outer_edge = edge_rows(tile(0), tile(5))
        inner_edge = jnp.where(
            (lane == 16) | (lane == 17),
            pltpu.roll(tile(3), 16, 1),
            jnp.where((lane == 30) | (lane == 31), pltpu.roll(tile(2), 32, 1), 0.0),
        )
        both = outer_edge + inner_edge
        picked = picked + (both if p == 0 else pltpu.roll(both, 32, 1))
    edges[0:64, :] = picked.T[0:64, :]
    edges[64:66, :] = radial_parts[:, 0:256]
    edges[66:68, :] = radial_parts[:, 512:768]
    edges[68:72, :] = jnp.zeros((4, CH), F32)
    row8 = lax.broadcasted_iota(jnp.int32, (8, CH), 0)
    slab = jnp.where(row8 < 4, edges[0:8, :], pltpu.roll(edges[32:40, :], 4, 0))
    slab = jnp.concatenate([slab[:, 0:128], slab[:, 128:256]], axis=0).astype(BF)

    for s, main in enumerate((m0, m1, m2, m3)):
        t = (me + s) & 3
        p = t >> 1
        h = t & 1
        base = pl.multiple_of(p * 32, 32)
        inside = edges[pl.ds(base + 16, 16), :].astype(BF)
        own = edges[pl.ds(base, 16), :].astype(BF)
        tails = (inside[:, 0:128], inside[:, 128:256], slab)
        ends = (own[:, 0:128], own[:, 128:256], slab)
        for m in range(3):
            start = (3 * h + m) * 2 + p
            main[PART * m : PART * m + CH, :] = u3[pl.ds(start, CH, stride=ROWS), :].astype(BF)
            main[PART * m + CH : PART * m + CH + 16, :] = tails[m]
            main[PART * m + CH + 16 : PART * (m + 1), :] = ends[m]


def couple_kernel(idx, field, m0, m1, m2, m3, beyond, comb_own, q1, q2, q3, low, high, labcol, radial_parts,
                  c0, c1, c2, c3, comb, pair, wide_u, both, laps, weights):
    me = idx[0]
    rad = idx[1]
    core = rad & 1
    p = me >> 1
    h = me & 1
    mains = (m0, m1, m2, m3)
    comb[:, 0:CH] = comb_own[...]
    ours = pl.ds(pl.multiple_of(core * 512, 512), 512)
    others = pl.ds(pl.multiple_of((1 - core) * 512, 512), 512)
    for s, (got, swapped) in enumerate(zip((m1, m2, m3), (q1, q2, q3)), 1):
        for half in range(2):
            at = s * CH + half * 128
            src = PIECE + 512 * half
            comb[ours, at : at + 128] = got[src : src + 512, :]
            comb[others, at : at + 128] = swapped[src : src + 512, :]
    wide = HALF + 128
    weights[...] = stencil(512, 256)
    for s in range(4):
        src = (me - s) & 3
        odd = parity(labcol[pl.ds(pl.multiple_of(src * CH, CH), CH), 0:1]).astype(F32)
        rows = slice(s * CH, (s + 1) * CH)
        main = mains[s]
        inside = jnp.concatenate([main[CH : CH + 16, :], main[PART + CH : PART + CH + 16, :]], axis=1).astype(F32)
        outside = beyond[:, pl.ds(pl.multiple_of(src * CH, CH), CH)].astype(F32)
        halo = halo_tile(jnp.where(h == 0, inside, outside), jnp.where(h == 0, outside, inside)).astype(BF)
        even16 = (1.0 - odd).astype(BF)
        odd16 = odd.astype(BF)
        tiles = [main[PART * m : PART * m + CH, :] for m in range(3)] + [halo]
        wide_u[rows, 0:128] = halo
        for m, tile in enumerate(tiles):
            wide_u[rows, 128 * (m + 1) : 128 * (m + 2)] = tile
            pair[rows, 128 * m : 128 * m + 128] = tile * even16
            pair[rows, wide + 128 * m : wide + 128 * m + 128] = tile * odd16
    for n in range(4):
        cols = slice(n * 256, n * 256 + 256)
        both[:, cols] = matmul(comb[...], pair[:, cols])
    laps[:, 0:256] = matmul(wide_u[:, 0:512], weights[...])
    laps[:, 256:HALF] = matmul(wide_u[:, 256:640], weights[0:384, 0:128])
    inv = inverse_square(rad * 768 + h * HALF, HALF)
    scale = jnp.where(p == 1, TAU, -TAU)
    cols = pl.ds(pl.multiple_of(h * HALF, 128), HALF)
    near = lanes((1, 128)) < 64
    row0 = jnp.concatenate(
        [radial_parts[0:1, cols], jnp.where(near, high[64:65, 0:128], low[66:67, 128:256])], axis=1) * field[0]
    row1 = jnp.concatenate(
        [radial_parts[1:2, cols], jnp.where(near, high[65:66, 0:128], low[67:68, 128:256])], axis=1)
    outs = (c0, c1, c2, c3)
    for target, out in enumerate(outs):
        t = (me + target) & 3
        s = (4 - target) % 4
        rows = pl.ds(pl.multiple_of(t * CH, CH), CH)
        spot = slice(s * CH, (s + 1) * CH)
        lab = labcol[rows, 0:1]
        even = parity(lab) == 0
        centrifugal = half_square(lab)
        for m in range(4):
            tile = slice(128 * m, 128 * m + 128)
            a, b = both[rows, tile], both[rows, wide + 128 * m : wide + 128 * m + 128]
            coupled = row1[:, tile] * jnp.where(even, a, b) + row0[:, tile] * jnp.where(even, b, a)
            out[:, tile] = coupled.astype(BF)
            if m < 3:
                u = wide_u[spot, 128 * (m + 1) : 128 * (m + 2)].astype(F32)
                value = scale * (coupled + (-0.5 / LAP) * laps[spot, tile] + centrifugal * inv[:, tile] * u)
                pair[spot, tile] = jnp.where(even, value, 0.0).astype(BF)
                pair[spot, HALF + 128 * m : HALF + 128 * m + 128] = jnp.where(even, 0.0, value).astype(BF)
    for n in range(3):
        cols = slice(n * 256, n * 256 + 256)
        both[:, cols] = matmul(comb[...], pair[:, cols])
    for target, out in enumerate(outs):
        t = (me + target) & 3
        rows = pl.ds(pl.multiple_of(t * CH, CH), CH)
        even = parity(labcol[rows, 0:1]) == 0
        for m in range(3):
            tile = slice(128 * m, 128 * m + 128)
            a, b = both[rows, tile], both[rows, HALF + 128 * m : HALF + 128 * m + 128]
            coupled = row1[:, tile] * jnp.where(even, a, b) + row0[:, tile] * jnp.where(even, b, a)
            out[:, wide + 128 * m : wide + 128 * m + 128] = coupled.astype(BF)


def split(x):
    high = x.astype(BF)
    return high, (x - high.astype(F32)).astype(BF)


def store_split(upper, lower, p, cols, x):
    upper[p, :, cols], lower[p, :, cols] = split(x)


def terms_kernel(idx, u3, low, high, c0, c1, c2, c3, labcol, first3, second3, state, kept, upper, lower, laps,
                 weights):
    me = idx[0]
    rad = idx[1]
    cs = (c0, c1, c2, c3)
    wide = HALF + 128
    weights[...] = stencil(512, 256)
    for p in range(2):
        halo = halo_tile(high[p * 32 : p * 32 + 16, :], low[p * 32 : p * 32 + 16, :])
        for tile in range(8):
            cols = slice(128 * tile, 128 * tile + 128)
            x = halo if tile in (0, 7) else u3[pl.ds(2 * (tile - 1) + p, CH, stride=ROWS), :]
            state[p, :, cols] = x
            store_split(upper, lower, p, cols, x)

    def window(p, start, depth, width):
        part = slice(start, start + depth)
        w = weights[0:depth, 0:width]
        return matmul(upper[p, :, part], w) + matmul(lower[p, :, part], w)

    for p in range(2):
        w = weights[128:384, 0:128]
        laps[p, :, 0:128] = matmul(upper[p, :, 0:256], w) + matmul(lower[p, :, 0:256], w)
        laps[p, :, 896:1024] = window(p, 768, 256, 128)
        for n in range(3):
            laps[p, :, 128 + 256 * n : 384 + 256 * n] = window(p, 256 * n, 512, 256)
    lab = labcol[pl.ds(pl.multiple_of(me * CH, CH), CH), 0:1]
    centrifugal = half_square(lab)

    for s in range(4):
        t = (me - s) & 3
        p = t >> 1
        h = t & 1
        scale = jnp.where(p == 1, TAU, -TAU)
        inv = inverse_square(rad * 768 + h * HALF, HALF)
        for m in range(4):
            if m < 3:
                cols = pl.ds(pl.multiple_of(h * HALF + 128 * (m + 1), 128), 128)
                tile_inv, tile_scale = inv[:, 128 * m : 128 * m + 128], scale
            else:
                cols = pl.ds(pl.multiple_of(h * 896, 128), 128)
                tile_inv = inverse_square(rad * 768 - 128 + h * 896, 128)
                tile_scale = scale
            coupled = cs[s][:, 128 * m : 128 * m + 128].astype(F32)
            value = tile_scale * (coupled + (-0.5 / LAP) * laps[p, :, cols] + centrifugal * tile_inv * state[p, :, cols])
            if m == 3:
                outside = ((rad == 0) & (h == 0)) | ((rad == 63) & (h == 1))
                value = jnp.where(outside, 0.0, value)
            kept[1 - p, :, cols] = value
            store_split(upper, lower, 1 - p, cols, value)
            if m < 3:
                first3[pl.ds((3 * h + m) * 2 + 1 - p, CH, stride=ROWS), :] = value

    for p in range(2):
        for n in range(3):
            laps[p, :, 128 + 256 * n : 384 + 256 * n] = window(p, 256 * n, 512, 256)
    for s in range(4):
        t = (me - s) & 3
        p = 1 - (t >> 1)
        h = t & 1
        scale = jnp.where(p == 1, 0.5 * TAU, -0.5 * TAU)
        inv = inverse_square(rad * 768 + h * HALF, HALF)
        for m in range(3):
            cols = pl.ds(pl.multiple_of(h * HALF + 128 * (m + 1), 128), 128)
            coupled = cs[s][:, wide + 128 * m : wide + 128 * m + 128].astype(F32)
            tile_inv = inv[:, 128 * m : 128 * m + 128]
            value = scale * (coupled + (-0.5 / LAP) * laps[p, :, cols] + centrifugal * tile_inv * kept[p, :, cols])
            second3[pl.ds((3 * h + m) * 2 + 1 - p, CH, stride=ROWS), :] = value


def split_couple(rows, comb, labels, me):
    odd = parity(labels[...]).astype(F32)
    from_even = jnp.dot((rows * (1.0 - odd)).astype(BF), comb[...], preferred_element_type=F32)
    from_odd = jnp.dot((rows * odd).astype(BF), comb[...], preferred_element_type=F32)
    mine_odd = parity(labels[:, pl.ds(pl.multiple_of(me * CH, CH), CH)]) == 1
    same = jnp.where(mine_odd, from_odd, from_even)
    other = jnp.where(mine_odd, from_even, from_odd)
    return same, other


def boundary_kernel(idx, field, m0, m1, m2, m3, comb, edges, labels, radial_parts, out, own, rows):
    me = idx[0]
    for s, main in enumerate((m0, m1, m2, m3)):
        src = (me - s) & 3
        block = main[2 * PART + CH : 2 * PART + CH + 16, :].astype(F32)
        at = pl.multiple_of(src * CH, CH)
        rows[:, pl.ds(at, 128)] = block[0:8]
        rows[:, pl.ds(at + 128, 128)] = block[8:16]
        for half in range(2):
            own[:, pl.ds(at + 128 * half, 128)] = main[PART * half + CH + 16 : PART * half + CH + 32, :]
    same, other = split_couple(rows[...], comb, labels, me)
    mine = labels[:, pl.ds(pl.multiple_of(me * CH, CH), CH)].astype(F32)
    image = []
    for p in range(2):
        w = [edges[p * 32 + j : p * 32 + j + 1, :] for j in range(5)]
        laps = (
            16.0 * w[1] - w[2] - 30.0 * w[0],
            16.0 * (w[0] + w[2]) - 30.0 * w[1] - w[3],
            16.0 * (w[1] + w[3]) - 30.0 * w[2] - w[0] - w[4],
        )
        terms = []
        for j in range(3):
            radius = INNER_RADIUS + (j + 1) * STEP
            r = p * 4 + j
            coupled = (field[0] * radial_parts[0:1, j : j + 1] * other[r : r + 1, :]
                       + radial_parts[1:2, j : j + 1] * same[r : r + 1, :])
            terms.append(-0.5 / LAP * laps[j] + half_square(mine) * (1.0 / (radius * radius)) * w[j] + coupled)
        image.append((4.0 * terms[1] - 3.0 * terms[0] - terms[2]) * (1.0 / (2.0 * STEP)))
    out[0:1, :] = TAU * image[1]
    out[1:2, :] = -TAU * image[0]


def ghost_image(g):
    image = [(-0.5 / LAP * (16.0 * g[p][1] - g[p][0]), 0.5 / LAP * g[p][1]) for p in range(2)]
    return [[TAU * image[1][j] for j in range(2)], [-TAU * image[0][j] for j in range(2)]]


def ghost_rows(ghosts, q):
    return [[ghosts[pl.ds((p * 2 + k) * 4 + q, 1), :] for k in range(2)] for p in range(2)]


def fix_kernel(idx, field, first_in, second_in, ghosts, b0, b1, b2, b3, comb, labels, radial_parts, first, second,
               rows):
    me = idx[0]
    on = jnp.where(idx[1] == 0, 1.0, 0.0)
    rows[...] = jnp.zeros((8, 1024), F32)
    for q in range(4):
        image = ghost_image(ghost_rows(ghosts, q))
        for p in range(2):
            for j in range(2):
                low = image[p][j].astype(BF).astype(F32)
                rows[p * 4 + j : p * 4 + j + 1, q * CH : (q + 1) * CH] = low
    same, other = split_couple(rows[...], comb, labels, me)
    mine = labels[:, pl.ds(pl.multiple_of(me * CH, CH), CH)].astype(F32)
    added = ghost_image(ghost_rows(ghosts, me))
    later = ((b0, b1), (b2, b3))
    images = []
    for p in range(2):
        g0, g1 = [jnp.concatenate([later[p][k][0:1, :], later[p][k][1:2, :]], axis=1) for k in range(2)]
        f0, f1 = added[p]
        laps = (16.0 * (f1 + g1) - 30.0 * f0 - g0, 16.0 * f0 - 30.0 * f1 - g1, 16.0 * f1 - f0, -f1)
        terms = [-0.5 / LAP * lap for lap in laps]
        for j in range(2):
            radius = INNER_RADIUS + (j + 1) * STEP
            r = p * 4 + j
            terms[j] = (terms[j] + half_square(mine) * (1.0 / (radius * radius)) * added[p][j]
                        + field[0] * radial_parts[0:1, j : j + 1] * other[r : r + 1, :]
                        + radial_parts[1:2, j : j + 1] * same[r : r + 1, :])
        images.append(terms)

    def columns(values):
        row = lax.broadcasted_iota(jnp.int32, (128, CH), 0)
        spread = jnp.zeros((128, CH), F32)
        for j, value in enumerate(values):
            spread = jnp.where(row == j, jnp.broadcast_to(value, (128, CH)), spread)
        return (spread * on).T

    for p in range(2):
        first[:, p, :] = first_in[:, p, :] + columns(added[p])
        sign = 0.5 * TAU if p == 0 else -0.5 * TAU
        second[:, p, :] = second_in[:, p, :] + columns([sign * term for term in images[1 - p]])


def active_row(idx, sizes):
    dev = idx[2]
    place = (dev & 7) * INNER + lanes((1, INNER))
    return (place < sizes[dev >> 3]).astype(F32)


def pad_row(row):
    return jnp.concatenate([row, jnp.zeros((row.shape[0], 128 - row.shape[1]), F32)], axis=1)


def low_rows(v):
    return jnp.concatenate([v, jnp.zeros((6, INNER), F32)], axis=0).astype(BF)


def fill(message, rows):
    tile = jnp.concatenate(rows, axis=0)
    message[...] = jnp.broadcast_to(tile[None], (NDEV, 8, 128)).reshape(NDEV * 8, 128)


def inner_prepare_kernel(idx, sizes, psi, edges, surface, out, now, message, table):
    v = psi[...] * active_row(idx, sizes)
    now[...] = v
    low = low_rows(v)
    slopes = []
    for p in range(2):
        w = [edges[p * 32 + j : p * 32 + j + 1, :] for j in range(3)]
        slope = (4.0 * w[1] - 3.0 * w[0] - w[2]) * (1.0 / (2.0 * STEP))
        slopes += [slope[:, 0:128], slope[:, 128:256]]
    lows = pad_row(v)
    fill(message, slopes + [lows[0:1], lows[1:2], jnp.zeros((2, 128), F32)])
    table[...] = jnp.zeros((128, CH), F32)
    for k in range(2):
        part = jnp.dot(low, surface[k], preferred_element_type=F32)
        for p in range(2):
            for q in range(4):
                at = (p * 2 + k) * 4 + q
                table[at : at + 1, :] = part[p : p + 1, q * CH : (q + 1) * CH]
    mine = table[...].T
    high = mine.astype(BF).astype(F32)
    message[pl.ds(6, NDEV, stride=8), :] = high + pltpu.roll(mine - high, 16, 1)
    out[...] = message[...].reshape(NDEV, 8, 128).astype(BF)


def dipole_copy(dipole, rows_held, arrived, b):
    cols = pl.ds(pl.multiple_of(b * BCAP, BCAP), BCAP)
    return pltpu.make_async_copy(dipole.at[:, cols], rows_held.at[:, cols], arrived.at[b])


def fetch_dipole(idx, links, dipole, rows_held, arrived):
    def step(b, _):
        @pl.when(links[idx[2] >> 3, b] != 0)
        def _():
            dipole_copy(dipole, rows_held, arrived, b).start()
        return 0

    lax.fori_loop(0, 32, step, 0)


def apply_inner(idx, field, sizes, links, energies, got, dipole, surface, v, slope_row, table, sums, rows_held,
                arrived):
    block = idx[2] >> 3
    lane = lanes((64, 128))
    for p in range(2):
        x = [got[pl.ds(4 + p + 8 * q, 64, stride=32), :] for q in range(4)]
        table[p, 0] = jnp.where(lane < 96, x[0], pltpu.roll(x[1], 96, 1))
        table[p, 1] = jnp.where(lane < 64, pltpu.roll(x[1], 96, 1), pltpu.roll(x[2], 64, 1))
        table[p, 2] = jnp.where(lane < 32, pltpu.roll(x[2], 64, 1), pltpu.roll(x[3], 32, 1))

    zero = jnp.zeros((INNER, 128), F32)
    for p in range(2):
        sums[p] = zero

    def step(b, _):
        @pl.when(links[block, b] != 0)
        def _():
            dipole_copy(dipole, rows_held, arrived, b).wait()
            totals = [zero, zero]
            for half in range(2):
                for m in range(3):
                    at = pl.multiple_of(b * BCAP + half * 384 + m * 128, 128)
                    tile = rows_held[:, pl.ds(at, 128)].astype(F32)
                    for p in range(2):
                        totals[p] = totals[p] + tile * table[p, m, pl.ds(2 * b + half, 1), :]
            for p in range(2):
                sums[p] = sums[p] + totals[p]
        return 0

    lax.fori_loop(0, 32, step, 0)
    rows = []
    for p in range(2):
        bloch = zero
        for block128 in range(8):
            tile = surface[1, :, block128 * 128 : block128 * 128 + 128].astype(F32)
            bloch = bloch + tile * slope_row(p, block128)
        total = field[0] * sums[p] + 0.5 * bloch
        total = jnp.concatenate([total, jnp.zeros((32, 128), F32)], axis=0)
        rows.append(jnp.sum(total.T, axis=0, keepdims=True)[:, 0:INNER])
    image = energies[...] * v + jnp.concatenate(rows, axis=0)
    return active_row(idx, sizes) * image


def turned(scale, image):
    return jnp.concatenate([scale * image[1:2], -scale * image[0:1]], axis=0)


def inner_first_kernel(idx, field, sizes, links, received, dipole, surface, now, energies, slope, out, term,
                       got, table, sums, rows_held, arrived, message):
    fetch_dipole(idx, links, dipole, rows_held, arrived)
    got[...] = received[...].astype(F32).reshape(NDEV * 8, 128)

    def slope_row(p, block128):
        src, half = block128 // 2, block128 % 2
        at = 8 * src + 2 * p + half
        return got[at : at + 1, :]

    image = apply_inner(idx, field, sizes, links, energies, got, dipole, surface, now[...], slope_row, table,
                        sums, rows_held, arrived)
    value = turned(TAU, image)
    term[...] = value
    low = low_rows(value)
    ghost = jnp.sum(got[pl.ds(6, NDEV, stride=8), :], axis=0, keepdims=True)
    ghost = ghost + pltpu.roll(ghost, 112, 1)
    ghost = jnp.where(lanes((1, 128)) < 16, ghost, 0.0)
    high = ghost.astype(BF).astype(F32)
    lows = pad_row(value)
    slopes = []
    for p in range(2):
        slopes += [slope[p : p + 1, 0:128], slope[p : p + 1, 128:256]]
    fill(message, slopes + [lows[0:1] + pltpu.roll(high, 96, 1), lows[1:2] + pltpu.roll(ghost - high, 96, 1),
                            jnp.zeros((2, 128), F32)])
    for k in range(2):
        part = jnp.dot(low, surface[k], preferred_element_type=F32)
        for p in range(2):
            for c in range(4):
                dest = (p * 2 + k) * 4 + c
                for half in range(2):
                    at = dest * 8 + 6 + half
                    lo = c * CH + half * 128
                    message[at : at + 1, :] = part[p : p + 1, lo : lo + 128]
    out[...] = message[...].reshape(NDEV, 8, 128).astype(BF)


def inner_second_kernel(idx, field, sizes, links, received, dipole, surface, first, energies, term, ghosts,
                        got, table, sums, rows_held, arrived, slopes):
    fetch_dipole(idx, links, dipole, rows_held, arrived)
    got[...] = received[...].astype(F32).reshape(NDEV * 8, 128)
    lane = lanes((NDEV, 128))
    pairs = jnp.where(lane < 112, got[pl.ds(4, NDEV, stride=8), :] + got[pl.ds(5, NDEV, stride=8), :], 0.0)
    ghosts[...] = pltpu.roll(pairs, 32, 1).T[0:16, :]
    for q in range(4):
        image = ghost_image(ghost_rows(ghosts, q))
        for p in range(2):
            extra = (4.0 * image[p][1] - 3.0 * image[p][0]) * (1.0 / (2.0 * STEP))
            for half in range(2):
                at = 8 * q + 2 * p + half
                total = got[at : at + 1, :] + extra[:, half * 128 : half * 128 + 128]
                row = p * 8 + q * 2 + half
                slopes[row : row + 1, :] = total.astype(BF).astype(F32)

    def slope_row(p, block128):
        return slopes[p * 8 + block128 : p * 8 + block128 + 1, :]

    image = apply_inner(idx, field, sizes, links, energies, got, dipole, surface, first[...], slope_row, table,
                        sums, rows_held, arrived)
    term[...] = turned(0.5 * TAU, image)


def body(psi_outer, psi_inner, couplings, radial_parts, labels, surface, dipole_inner, energies, block_sizes,
         block_links, field):
    me = lax.axis_index("chan")
    rad = lax.axis_index("radial")
    idx = jnp.stack([me, rad, rad * NCHAN + me, jnp.zeros_like(me)]).astype(jnp.int32)
    everyone = ("radial", "chan")
    count = 64

    def chan_shift(x, s):
        return lax.ppermute(x, "chan", [(i, (i + s) % NCHAN) for i in range(NCHAN)])

    def core_swap(x):
        return lax.ppermute(x, "radial", [(i, i ^ 1) for i in range(count)])

    def edge_shift(x):
        pairs = []
        for r in range(count):
            for c in range(NCHAN):
                to, t = (r - 1, c + 1) if c % 2 == 0 else (r + 1, c - 1)
                if 0 <= to < count:
                    pairs.append((r * NCHAN + c, to * NCHAN + t))
        return lax.ppermute(x, everyone, pairs)

    def sector_shift(x):
        low = lax.ppermute(x, "radial", [(i, i + 1) for i in range(count - 1)])
        high = lax.ppermute(x, "radial", [(i + 1, i) for i in range(count - 1)])
        return low, high

    def exchange(x):
        return lax.all_to_all(x, everyone, 0, 0, tiled=True)

    tiles_first = Layout(major_to_minor=(0, 2, 1, 3))

    def flat(x):
        x = with_layout_constraint(x.reshape(CH, 2, 6, 128), tiles_first)
        return x.transpose(0, 2, 1, 3).reshape(CH * ROWS, 128)

    def unflat(x):
        x = with_layout_constraint(x.reshape(CH, 6, 2, 128).transpose(0, 2, 1, 3), tiles_first)
        return x.reshape(CH, 2, 768)

    u3 = flat(psi_outer)
    lab = labels.reshape(1, 1024)
    surf = jnp.swapaxes(surface, 1, 2)
    energy = energies.reshape(1, INNER)
    pack_shape = sds((PIECE + 1024, 128), BF)
    piece = sds((CH, 2 * HALF + 128), BF)

    prepared = call(
        prepare_kernel,
        (sds((PIECE, 128), BF),) + (pack_shape,) * 3
        + (sds((72, CH), F32), sds((1024, 128), F32), sds((1024, CH), BF)),
        [SMEM, VMEM, VMEM, VMEM, VMEM], (idx, u3, couplings, lab, radial_parts), name="prepare")
    packs = prepared[0:4]
    edges, labcol, comb_own = prepared[4:]

    got = {s: chan_shift(packs[s], s) for s in (2, 1, 3)}
    mains = (packs[0], got[1], got[2], got[3])

    message1, now = call(
        inner_prepare_kernel, (sds((NDEV, 8, 128), BF), sds((2, INNER), F32)),
        [SMEM, SMEM, VMEM, VMEM, VMEM], (idx, block_sizes, psi_inner, edges, surf),
        [pltpu.VMEM((NDEV * 8, 128), F32), pltpu.VMEM((128, CH), F32)], name="inner_prepare")
    received1 = exchange(message1)
    edges, now = lax.optimization_barrier((edges, now))
    low, high = sector_shift(edges)
    mains, low, high = lax.optimization_barrier((mains, low, high))

    slope, own = call(
        boundary_kernel, (sds((2, CH), F32), sds((16, 1024), BF)), [SMEM, SMEM] + [VMEM] * 8,
        (idx, field, *mains, comb_own, edges, lab, radial_parts),
        [pltpu.VMEM((8, 1024), F32)], name="boundary", flops=BOUNDARY_FLOPS)
    swapped = {s: core_swap(mains[s]) for s in (1, 3, 2)}
    beyond = edge_shift(own)

    pieces = call(
        couple_kernel, (piece,) * 4, [SMEM, SMEM] + [VMEM] * 13,
        (idx, field, *mains, beyond, comb_own, swapped[1], swapped[2], swapped[3], low, high, labcol,
         radial_parts),
        [pltpu.VMEM((1024, 1024), BF), pltpu.VMEM((1024, 1024), BF), pltpu.VMEM((1024, 640), BF),
         pltpu.VMEM((1024, 1024), F32), pltpu.VMEM((1024, HALF), F32), pltpu.VMEM((512, 256), BF)], name="couple")
    received1, pieces = lax.optimization_barrier((received1, pieces))
    back = [pieces[0]] + [chan_shift(pieces[s], s) for s in (1, 2, 3)]

    inner_scratch = [
        pltpu.VMEM((NDEV * 8, 128), F32), pltpu.VMEM((2, 3, 64, 128), F32), pltpu.VMEM((2, INNER, 128), F32),
        pltpu.VMEM((INNER, 32 * BCAP), BF), pltpu.SemaphoreType.DMA((32,))]
    message2, inner_first = call(
        inner_first_kernel, (sds((NDEV, 8, 128), BF), sds((2, INNER), F32)),
        [SMEM] * 4 + [VMEM, ANY] + [VMEM] * 4,
        (idx, field, block_sizes, block_links, received1, dipole_inner, surf, now, energy, slope),
        inner_scratch + [pltpu.VMEM((NDEV * 8, 128), F32)], name="inner_first")
    received2 = exchange(message2)

    sums = jnp.sum(received2[:, 6:8, :].astype(F32), axis=0)
    later = [sums] + [lax.ppermute(sums, "radial", [(j, 0)]) for j in (1, 2, 3)]

    inner_second, ghosts = call(
        inner_second_kernel, (sds((2, INNER), F32), sds((16, CH), F32)), [SMEM] * 4 + [VMEM, ANY] + [VMEM] * 3,
        (idx, field, block_sizes, block_links, received2, dipole_inner, surf, inner_first, energy),
        inner_scratch + [pltpu.VMEM((16, 128), F32)], name="inner_second")

    back, ghosts = lax.optimization_barrier((back, ghosts))
    first3, second3 = call(
        terms_kernel, (sds((CH * ROWS, 128), F32),) * 2, [SMEM] + [VMEM] * 8,
        (idx, u3, low, high, *back, labcol),
        [pltpu.VMEM((2, CH, 1024), F32)] * 2 + [pltpu.VMEM((2, CH, 1024), BF)] * 2
        + [pltpu.VMEM((2, CH, 1024), F32), pltpu.VMEM((512, 256), BF)], name="terms")

    tile = pl.BlockSpec((CH, 2, 128), lambda i: (0, 0, 0))
    outer_shape = sds((CH, 2, 768), F32)
    outer_first, outer_second = pl.pallas_call(
        fix_kernel, out_shape=(outer_shape, outer_shape), grid=(1,),
        in_specs=[SMEM, SMEM, tile, tile] + [VMEM] * 8, out_specs=(tile, tile),
        scratch_shapes=[pltpu.VMEM((8, 1024), F32)], input_output_aliases={2: 0, 3: 1}, name="fix",
        cost_estimate=pl.CostEstimate(flops=0, bytes_accessed=0, transcendentals=0),
        compiler_params=pltpu.CompilerParams(vmem_limit_bytes=60 << 20),
    )(idx, field, unflat(first3), unflat(second3), ghosts, *later, comb_own, lab, radial_parts)
    return outer_first, outer_second, inner_first, inner_second


def solution(mesh):
    in_specs = (
        P("chan", None, "radial"),
        P(None, ("radial", "chan")),
        P(None, None, "chan"),
        P(None, "radial"),
        P(),
        P(None, None, ("radial", "chan")),
        P(("radial", "chan"), None),
        P(("radial", "chan")),
        P(),
        P(),
        P(),
    )
    out_specs = (
        P("chan", None, "radial"),
        P("chan", None, "radial"),
        P(None, ("radial", "chan")),
        P(None, ("radial", "chan")),
    )
    return jax.shard_map(body, mesh=mesh, in_specs=in_specs, out_specs=out_specs, check_vma=False)
```

```python
import functools

import jax
import jax.numpy as jnp
from jax import lax
from jax.experimental import pallas as pl
from jax.experimental.pallas import tpu as pltpu
from jax.experimental.layout import Layout, with_layout_constraint
from jax.sharding import PartitionSpec as P

STEP = 0.2
INNER_RADIUS = 20.0
TAU = 0.025
LAP = 12.0 * STEP * STEP

CH = 256
ROWS = 12
NCHAN = 4
NDEV = 256
INNER = 96
HALF = 384
PART = CH + 32
PIECE = 3 * PART
BCAP = 768
BOUNDARY_FLOPS = 10**10
BESIDE_FLOPS = 3 * 10**10

BF = jnp.bfloat16
F32 = jnp.float32
VMEM = pl.BlockSpec(memory_space=pltpu.VMEM)
SMEM = pl.BlockSpec(memory_space=pltpu.SMEM)
ANY = pl.BlockSpec(memory_space=pl.ANY)


def sds(shape, dtype):
    return jax.ShapeDtypeStruct(shape, dtype)


def call(kernel, out_shape, specs, args, scratch=(), name=None, flops=0, limit=60):
    return pl.pallas_call(
        kernel,
        out_shape=out_shape,
        in_specs=specs,
        out_specs=jax.tree.map(lambda _: VMEM, out_shape),
        scratch_shapes=list(scratch),
        name=name,
        cost_estimate=pl.CostEstimate(flops=flops, bytes_accessed=0, transcendentals=0),
        compiler_params=pltpu.CompilerParams(vmem_limit_bytes=limit << 20),
    )(*args)


def lanes(shape):
    return lax.broadcasted_iota(jnp.int32, shape, len(shape) - 1)


def stencil(depth, width):
    gap = jnp.abs(lax.broadcasted_iota(jnp.int32, (depth, width), 0) - lanes((depth, width)) - 128)
    weight = jnp.where(gap == 0, -30.0, jnp.where(gap == 1, 16.0, jnp.where(gap == 2, -1.0, 0.0)))
    return weight.astype(BF)


def matmul(a, b):
    return jnp.dot(a, b, preferred_element_type=F32)


def inverse_square(start, width):
    pos = start + lanes((1, width))
    radius = INNER_RADIUS + (pos + 1).astype(F32) * STEP
    return 1.0 / (radius * radius)


def half_square(lab):
    return lab * (lab + 1.0) * 0.5


def parity(lab):
    return lab.astype(jnp.int32) & 1


def halo_tile(right, left):
    rows = jnp.concatenate([right, jnp.zeros((96, CH), F32), left], axis=0)
    return rows.T


def edge_rows(tile0, tile5):
    lane = lanes((CH, 128))
    return jnp.where(lane < 5, tile0, jnp.where((lane >= 12) & (lane < 16), pltpu.roll(tile5, 16, 1), 0.0))


def prepare_kernel(idx, u3, couplings, labels, radial_parts, m0, m1, m2, m3, edges, labcol, comb):
    me = idx[0]
    core = idx[1] & 1
    lab_rows = jnp.broadcast_to(labels[...].astype(F32), (128, 1024))
    labcol[...] = lab_rows.T
    mine = labels[:, pl.ds(pl.multiple_of(me * CH, CH), CH)].astype(F32)
    for part in range(4):
        rows = pl.ds(part * 256, 256)
        gap = jnp.abs(labcol[rows, 0:1] - mine)
        zero = couplings[0, rows, :].astype(F32)
        one = couplings[1, rows, :].astype(F32)
        value = jnp.where(gap == 1.0, zero, jnp.where((gap == 0.0) | (gap == 2.0), one, 0.0))
        comb[rows, :] = value.astype(BF)
    half = comb[pl.ds(pl.multiple_of(core * 512, 512), 512), :]
    for pack in (m1, m2, m3):
        pack[PIECE : PIECE + 512, :] = half[:, 0:128]
        pack[PIECE + 512 : PIECE + 1024, :] = half[:, 128:256]

    lane = lanes((CH, 128))
    picked = jnp.zeros((CH, 128), F32)
    for p in range(2):
        def tile(jb):
            return u3[pl.ds(2 * jb + p, CH, stride=ROWS), :]
        outer_edge = edge_rows(tile(0), tile(5))
        inner_edge = jnp.where(
            (lane == 16) | (lane == 17),
            pltpu.roll(tile(3), 16, 1),
            jnp.where((lane == 30) | (lane == 31), pltpu.roll(tile(2), 32, 1), 0.0),
        )
        both = outer_edge + inner_edge
        picked = picked + (both if p == 0 else pltpu.roll(both, 32, 1))
    edges[0:64, :] = picked.T[0:64, :]
    edges[64:66, :] = radial_parts[:, 0:256]
    edges[66:68, :] = radial_parts[:, 512:768]
    edges[68:72, :] = jnp.zeros((4, CH), F32)
    row8 = lax.broadcasted_iota(jnp.int32, (8, CH), 0)
    slab = jnp.where(row8 < 4, edges[0:8, :], pltpu.roll(edges[32:40, :], 4, 0))
    slab = jnp.concatenate([slab[:, 0:128], slab[:, 128:256]], axis=0).astype(BF)

    for s, main in enumerate((m0, m1, m2, m3)):
        t = (me + s) & 3
        p = t >> 1
        h = t & 1
        base = pl.multiple_of(p * 32, 32)
        inside = edges[pl.ds(base + 16, 16), :].astype(BF)
        own = edges[pl.ds(base, 16), :].astype(BF)
        tails = (inside[:, 0:128], inside[:, 128:256], slab)
        ends = (own[:, 0:128], own[:, 128:256], slab)
        for m in range(3):
            start = (3 * h + m) * 2 + p
            main[PART * m : PART * m + CH, :] = u3[pl.ds(start, CH, stride=ROWS), :].astype(BF)
            main[PART * m + CH : PART * m + CH + 16, :] = tails[m]
            main[PART * m + CH + 16 : PART * (m + 1), :] = ends[m]


def assemble(core, comb_own, own_half, other_half, comb):
    comb[:, 0:CH] = comb_own[...]
    ours = pl.ds(pl.multiple_of(core * 512, 512), 512)
    others = pl.ds(pl.multiple_of((1 - core) * 512, 512), 512)
    for s, (got, swapped) in enumerate(zip(own_half, other_half), 1):
        for half in range(2):
            at = s * CH + half * 128
            src = PIECE + 512 * half
            comb[ours, at : at + 128] = got[src : src + 512, :]
            comb[others, at : at + 128] = swapped[src : src + 512, :]


def couple_kernel(idx, field, m0, m1, m2, m3, beyond, comb_own, q1, q2, q3, low, high, labcol, radial_parts,
                  c0, c1, c2, c3, pair2, comb, pair, wide_u, both, laps, weights):
    me = idx[0]
    rad = idx[1]
    core = rad & 1
    p = me >> 1
    h = me & 1
    mains = (m0, m1, m2, m3)
    assemble(core, comb_own, (m1, m2, m3), (q1, q2, q3), comb)
    wide = HALF + 128
    weights[...] = stencil(512, 256)
    for s in range(4):
        src = (me - s) & 3
        odd = parity(labcol[pl.ds(pl.multiple_of(src * CH, CH), CH), 0:1]).astype(F32)
        rows = slice(s * CH, (s + 1) * CH)
        main = mains[s]
        inside = jnp.concatenate([main[CH : CH + 16, :], main[PART + CH : PART + CH + 16, :]], axis=1).astype(F32)
        outside = beyond[:, pl.ds(pl.multiple_of(src * CH, CH), CH)].astype(F32)
        halo = halo_tile(jnp.where(h == 0, inside, outside), jnp.where(h == 0, outside, inside)).astype(BF)
        even16 = (1.0 - odd).astype(BF)
        odd16 = odd.astype(BF)
        tiles = [main[PART * m : PART * m + CH, :] for m in range(3)] + [halo]
        wide_u[rows, 0:128] = halo
        for m, tile in enumerate(tiles):
            wide_u[rows, 128 * (m + 1) : 128 * (m + 2)] = tile
            pair[rows, 128 * m : 128 * m + 128] = tile * even16
            pair[rows, wide + 128 * m : wide + 128 * m + 128] = tile * odd16
    for n in range(4):
        cols = slice(n * 256, n * 256 + 256)
        both[:, cols] = matmul(comb[...], pair[:, cols])
    laps[:, 0:256] = matmul(wide_u[:, 0:512], weights[...])
    laps[:, 256:HALF] = matmul(wide_u[:, 256:640], weights[0:384, 0:128])
    inv = inverse_square(rad * 768 + h * HALF, HALF)
    scale = jnp.where(p == 1, TAU, -TAU)
    cols = pl.ds(pl.multiple_of(h * HALF, 128), HALF)
    near = lanes((1, 128)) < 64
    row0 = jnp.concatenate(
        [radial_parts[0:1, cols], jnp.where(near, high[64:65, 0:128], low[66:67, 128:256])], axis=1) * field[0]
    row1 = jnp.concatenate(
        [radial_parts[1:2, cols], jnp.where(near, high[65:66, 0:128], low[67:68, 128:256])], axis=1)
    outs = (c0, c1, c2, c3)
    for target, out in enumerate(outs):
        t = (me + target) & 3
        s = (4 - target) % 4
        rows = pl.ds(pl.multiple_of(t * CH, CH), CH)
        spot = slice(s * CH, (s + 1) * CH)
        lab = labcol[rows, 0:1]
        even = parity(lab) == 0
        centrifugal = half_square(lab)
        for m in range(4):
            tile = slice(128 * m, 128 * m + 128)
            a, b = both[rows, tile], both[rows, wide + 128 * m : wide + 128 * m + 128]
            coupled = row1[:, tile] * jnp.where(even, a, b) + row0[:, tile] * jnp.where(even, b, a)
            out[:, tile] = coupled.astype(BF)
            if m < 3:
                u = wide_u[spot, 128 * (m + 1) : 128 * (m + 2)].astype(F32)
                value = scale * (coupled + (-0.5 / LAP) * laps[spot, tile] + centrifugal * inv[:, tile] * u)
                pair2[spot, tile] = jnp.where(even, value, 0.0).astype(BF)
                pair2[spot, HALF + 128 * m : HALF + 128 * m + 128] = jnp.where(even, 0.0, value).astype(BF)


def couple_again_kernel(idx, field, m1, m2, m3, comb_own, q1, q2, q3, labcol, radial_parts, pair2,
                        c0, c1, c2, c3, comb, both):
    me = idx[0]
    assemble(idx[1] & 1, comb_own, (m1, m2, m3), (q1, q2, q3), comb)
    for n in range(3):
        cols = slice(n * 256, n * 256 + 256)
        both[:, cols] = matmul(comb[...], pair2[:, cols])
    cols = pl.ds(pl.multiple_of((me & 1) * HALF, 128), HALF)
    row0 = radial_parts[0:1, cols] * field[0]
    row1 = radial_parts[1:2, cols]
    for target, out in enumerate((c0, c1, c2, c3)):
        t = (me + target) & 3
        rows = pl.ds(pl.multiple_of(t * CH, CH), CH)
        even = parity(labcol[rows, 0:1]) == 0
        for m in range(3):
            tile = slice(128 * m, 128 * m + 128)
            a, b = both[rows, tile], both[rows, HALF + 128 * m : HALF + 128 * m + 128]
            coupled = row1[:, tile] * jnp.where(even, a, b) + row0[:, tile] * jnp.where(even, b, a)
            out[:, tile] = coupled.astype(BF)


def split(x):
    high = x.astype(BF)
    return high, (x - high.astype(F32)).astype(BF)


def store_split(upper, lower, p, cols, x):
    upper[p, :, cols], lower[p, :, cols] = split(x)


def stencil_window(upper, lower, weights, p, start, depth, width):
    part = slice(start, start + depth)
    w = weights[0:depth, 0:width]
    return matmul(upper[p, :, part], w) + matmul(lower[p, :, part], w)


def load_state(source3, halos, state, upper, lower, laps, weights):
    for p in range(2):
        for tile in range(8):
            cols = slice(128 * tile, 128 * tile + 128)
            x = halos[p] if tile in (0, 7) else source3[pl.ds(2 * (tile - 1) + p, CH, stride=ROWS), :]
            state[p, :, cols] = x
            store_split(upper, lower, p, cols, x)
    for p in range(2):
        for n in range(3):
            laps[p, :, 128 + 256 * n : 384 + 256 * n] = stencil_window(upper, lower, weights, p, 256 * n, 512, 256)


def first_term_kernel(idx, u3, low, high, c0, c1, c2, c3, labcol, first3, sides, state, upper, lower, laps, weights,
                      side):
    me = idx[0]
    rad = idx[1]
    cs = (c0, c1, c2, c3)
    weights[...] = stencil(512, 256)
    halos = [halo_tile(high[p * 32 : p * 32 + 16, :], low[p * 32 : p * 32 + 16, :]) for p in range(2)]
    load_state(u3, halos, state, upper, lower, laps, weights)
    for p in range(2):
        w = weights[128:384, 0:128]
        laps[p, :, 0:128] = matmul(upper[p, :, 0:256], w) + matmul(lower[p, :, 0:256], w)
        laps[p, :, 896:1024] = stencil_window(upper, lower, weights, p, 768, 256, 128)
    lab = labcol[pl.ds(pl.multiple_of(me * CH, CH), CH), 0:1]
    centrifugal = half_square(lab)
    left = lanes((CH, 128)) >= 64
    for s in range(4):
        t = (me - s) & 3
        p = t >> 1
        h = t & 1
        scale = jnp.where(p == 1, TAU, -TAU)
        inv = inverse_square(rad * 768 + h * HALF, HALF)
        for m in range(4):
            if m < 3:
                cols = pl.ds(pl.multiple_of(h * HALF + 128 * (m + 1), 128), 128)
                tile_inv = inv[:, 128 * m : 128 * m + 128]
            else:
                cols = pl.ds(pl.multiple_of(h * 896, 128), 128)
                tile_inv = inverse_square(rad * 768 - 128 + h * 896, 128)
            coupled = cs[s][:, 128 * m : 128 * m + 128].astype(F32)
            value = scale * (coupled + (-0.5 / LAP) * laps[p, :, cols] + centrifugal * tile_inv * state[p, :, cols])
            if m < 3:
                first3[pl.ds((3 * h + m) * 2 + 1 - p, CH, stride=ROWS), :] = value
            else:
                outside = ((rad == 0) & (h == 0)) | ((rad == 63) & (h == 1))
                side[1 - p, :, pl.ds(pl.multiple_of(128 * h, 128), 128)] = jnp.where(outside, 0.0, value)
    for p in range(2):
        sides[p] = jnp.where(left, side[p, :, 0:128], side[p, :, 128:256])


def second_term_kernel(idx, first3, sides, c0, c1, c2, c3, labcol, second3, state, upper, lower, laps, weights):
    me = idx[0]
    rad = idx[1]
    weights[...] = stencil(512, 256)
    load_state(first3, (sides[0], sides[1]), state, upper, lower, laps, weights)
    centrifugal = half_square(labcol[pl.ds(pl.multiple_of(me * CH, CH), CH), 0:1])
    for s, c in enumerate((c0, c1, c2, c3)):
        t = (me - s) & 3
        p = 1 - (t >> 1)
        h = t & 1
        scale = jnp.where(p == 1, 0.5 * TAU, -0.5 * TAU)
        inv = inverse_square(rad * 768 + h * HALF, HALF)
        for m in range(3):
            tile = slice(128 * m, 128 * m + 128)
            cols = pl.ds(pl.multiple_of(h * HALF + 128 * (m + 1), 128), 128)
            value = scale * (c[:, tile].astype(F32) + (-0.5 / LAP) * laps[p, :, cols]
                             + centrifugal * inv[:, tile] * state[p, :, cols])
            second3[pl.ds((3 * h + m) * 2 + 1 - p, CH, stride=ROWS), :] = value


def split_couple(rows, comb, labels, me):
    odd = parity(labels[...]).astype(F32)
    from_even = jnp.dot((rows * (1.0 - odd)).astype(BF), comb[...], preferred_element_type=F32)
    from_odd = jnp.dot((rows * odd).astype(BF), comb[...], preferred_element_type=F32)
    mine_odd = parity(labels[:, pl.ds(pl.multiple_of(me * CH, CH), CH)]) == 1
    same = jnp.where(mine_odd, from_odd, from_even)
    other = jnp.where(mine_odd, from_even, from_odd)
    return same, other


def boundary_kernel(idx, field, a0, b0, t0, a1, b1, t1, a2, b2, t2, a3, b3, t3, comb, edges, labels, radial_parts, out, own, rows):
    me = idx[0]
    tails = ((a0, b0, t0), (a1, b1, t1), (a2, b2, t2), (a3, b3, t3))
    for s, (ends0, ends1, slab) in enumerate(tails):
        src = (me - s) & 3
        block = slab[0:16, :].astype(F32)
        at = pl.multiple_of(src * CH, CH)
        rows[:, pl.ds(at, 128)] = block[0:8]
        rows[:, pl.ds(at + 128, 128)] = block[8:16]
        own[:, pl.ds(at, 128)] = ends0[16:32, :]
        own[:, pl.ds(at + 128, 128)] = ends1[16:32, :]
    same, other = split_couple(rows[...], comb, labels, me)
    mine = labels[:, pl.ds(pl.multiple_of(me * CH, CH), CH)].astype(F32)
    image = []
    for p in range(2):
        w = [edges[p * 32 + j : p * 32 + j + 1, :] for j in range(5)]
        laps = (
            16.0 * w[1] - w[2] - 30.0 * w[0],
            16.0 * (w[0] + w[2]) - 30.0 * w[1] - w[3],
            16.0 * (w[1] + w[3]) - 30.0 * w[2] - w[0] - w[4],
        )
        terms = []
        for j in range(3):
            radius = INNER_RADIUS + (j + 1) * STEP
            r = p * 4 + j
            coupled = (field[0] * radial_parts[0:1, j : j + 1] * other[r : r + 1, :]
                       + radial_parts[1:2, j : j + 1] * same[r : r + 1, :])
            terms.append(-0.5 / LAP * laps[j] + half_square(mine) * (1.0 / (radius * radius)) * w[j] + coupled)
        image.append((4.0 * terms[1] - 3.0 * terms[0] - terms[2]) * (1.0 / (2.0 * STEP)))
    out[0:1, :] = TAU * image[1]
    out[1:2, :] = -TAU * image[0]


def ghost_image(g):
    image = [(-0.5 / LAP * (16.0 * g[p][1] - g[p][0]), 0.5 / LAP * g[p][1]) for p in range(2)]
    return [[TAU * image[1][j] for j in range(2)], [-TAU * image[0][j] for j in range(2)]]


def ghost_rows(ghosts, q):
    return [[ghosts[pl.ds((p * 2 + k) * 4 + q, 1), :] for k in range(2)] for p in range(2)]


def fix_kernel(idx, field, first_in, second_in, ghosts, b0, b1, b2, b3, comb, labels, radial_parts, first, second,
               rows):
    me = idx[0]
    on = jnp.where(idx[1] == 0, 1.0, 0.0)
    rows[...] = jnp.zeros((8, 1024), F32)
    for q in range(4):
        image = ghost_image(ghost_rows(ghosts, q))
        for p in range(2):
            for j in range(2):
                low = image[p][j].astype(BF).astype(F32)
                rows[p * 4 + j : p * 4 + j + 1, q * CH : (q + 1) * CH] = low
    same, other = split_couple(rows[...], comb, labels, me)
    mine = labels[:, pl.ds(pl.multiple_of(me * CH, CH), CH)].astype(F32)
    added = ghost_image(ghost_rows(ghosts, me))
    later = ((b0, b1), (b2, b3))
    images = []
    for p in range(2):
        g0, g1 = [jnp.concatenate([later[p][k][0:1, :], later[p][k][1:2, :]], axis=1) for k in range(2)]
        f0, f1 = added[p]
        laps = (16.0 * (f1 + g1) - 30.0 * f0 - g0, 16.0 * f0 - 30.0 * f1 - g1, 16.0 * f1 - f0, -f1)
        terms = [-0.5 / LAP * lap for lap in laps]
        for j in range(2):
            radius = INNER_RADIUS + (j + 1) * STEP
            r = p * 4 + j
            terms[j] = (terms[j] + half_square(mine) * (1.0 / (radius * radius)) * added[p][j]
                        + field[0] * radial_parts[0:1, j : j + 1] * other[r : r + 1, :]
                        + radial_parts[1:2, j : j + 1] * same[r : r + 1, :])
        images.append(terms)

    def columns(values):
        row = lax.broadcasted_iota(jnp.int32, (128, CH), 0)
        spread = jnp.zeros((128, CH), F32)
        for j, value in enumerate(values):
            spread = jnp.where(row == j, jnp.broadcast_to(value, (128, CH)), spread)
        return (spread * on).T

    for p in range(2):
        first[:, p, :] = first_in[:, p, :] + columns(added[p])
        sign = 0.5 * TAU if p == 0 else -0.5 * TAU
        second[:, p, :] = second_in[:, p, :] + columns([sign * term for term in images[1 - p]])


def active_row(idx, sizes):
    dev = idx[2]
    place = (dev & 7) * INNER + lanes((1, INNER))
    return (place < sizes[dev >> 3]).astype(F32)


def pad_row(row):
    return jnp.concatenate([row, jnp.zeros((row.shape[0], 128 - row.shape[1]), F32)], axis=1)


def low_rows(v):
    return jnp.concatenate([v, jnp.zeros((6, INNER), F32)], axis=0).astype(BF)


def fill(message, rows):
    tile = jnp.concatenate(rows, axis=0)
    message[...] = jnp.broadcast_to(tile[None], (NDEV, 8, 128)).reshape(NDEV * 8, 128)


def inner_prepare_kernel(idx, sizes, psi, edges, surface, out, now, message, table):
    v = psi[...] * active_row(idx, sizes)
    now[...] = v
    low = low_rows(v)
    slopes = []
    for p in range(2):
        w = [edges[p * 32 + j : p * 32 + j + 1, :] for j in range(3)]
        slope = (4.0 * w[1] - 3.0 * w[0] - w[2]) * (1.0 / (2.0 * STEP))
        slopes += [slope[:, 0:128], slope[:, 128:256]]
    lows = pad_row(v)
    fill(message, slopes + [lows[0:1], lows[1:2], jnp.zeros((2, 128), F32)])
    table[...] = jnp.zeros((128, CH), F32)
    for k in range(2):
        part = jnp.dot(low, surface[k], preferred_element_type=F32)
        for p in range(2):
            for q in range(4):
                at = (p * 2 + k) * 4 + q
                table[at : at + 1, :] = part[p : p + 1, q * CH : (q + 1) * CH]
    mine = table[...].T
    high = mine.astype(BF).astype(F32)
    message[pl.ds(6, NDEV, stride=8), :] = high + pltpu.roll(mine - high, 16, 1)
    out[...] = message[...].reshape(NDEV, 8, 128).astype(BF)


def dipole_copy(dipole, rows_held, arrived, b):
    cols = pl.ds(pl.multiple_of(b * BCAP, BCAP), BCAP)
    return pltpu.make_async_copy(dipole.at[:, cols], rows_held.at[:, cols], arrived.at[b])


def fetch_dipole(idx, links, dipole, rows_held, arrived):
    def step(b, _):
        @pl.when(links[idx[2] >> 3, b] != 0)
        def _():
            dipole_copy(dipole, rows_held, arrived, b).start()
        return 0

    lax.fori_loop(0, 32, step, 0)


def apply_inner(idx, field, sizes, links, energies, got, dipole, surface, v, slope_row, table, sums, rows_held,
                arrived):
    block = idx[2] >> 3
    lane = lanes((64, 128))
    for p in range(2):
        x = [got[pl.ds(4 + p + 8 * q, 64, stride=32), :] for q in range(4)]
        table[p, 0] = jnp.where(lane < 96, x[0], pltpu.roll(x[1], 96, 1))
        table[p, 1] = jnp.where(lane < 64, pltpu.roll(x[1], 96, 1), pltpu.roll(x[2], 64, 1))
        table[p, 2] = jnp.where(lane < 32, pltpu.roll(x[2], 64, 1), pltpu.roll(x[3], 32, 1))

    zero = jnp.zeros((INNER, 128), F32)
    for p in range(2):
        sums[p] = zero

    def step(b, _):
        @pl.when(links[block, b] != 0)
        def _():
            dipole_copy(dipole, rows_held, arrived, b).wait()
            totals = [zero, zero]
            for half in range(2):
                for m in range(3):
                    at = pl.multiple_of(b * BCAP + half * 384 + m * 128, 128)
                    tile = rows_held[:, pl.ds(at, 128)].astype(F32)
                    for p in range(2):
                        totals[p] = totals[p] + tile * table[p, m, pl.ds(2 * b + half, 1), :]
            for p in range(2):
                sums[p] = sums[p] + totals[p]
        return 0

    lax.fori_loop(0, 32, step, 0)
    rows = []
    for p in range(2):
        bloch = zero
        for block128 in range(8):
            tile = surface[1, :, block128 * 128 : block128 * 128 + 128].astype(F32)
            bloch = bloch + tile * slope_row(p, block128)
        total = field[0] * sums[p] + 0.5 * bloch
        total = jnp.concatenate([total, jnp.zeros((32, 128), F32)], axis=0)
        rows.append(jnp.sum(total.T, axis=0, keepdims=True)[:, 0:INNER])
    image = energies[...] * v + jnp.concatenate(rows, axis=0)
    return active_row(idx, sizes) * image


def turned(scale, image):
    return jnp.concatenate([scale * image[1:2], -scale * image[0:1]], axis=0)


def inner_first_kernel(idx, field, sizes, links, received, dipole, surface, now, energies, slope, out, term,
                       got, table, sums, rows_held, arrived, message):
    fetch_dipole(idx, links, dipole, rows_held, arrived)
    got[...] = received[...].astype(F32).reshape(NDEV * 8, 128)

    def slope_row(p, block128):
        src, half = block128 // 2, block128 % 2
        at = 8 * src + 2 * p + half
        return got[at : at + 1, :]

    image = apply_inner(idx, field, sizes, links, energies, got, dipole, surface, now[...], slope_row, table,
                        sums, rows_held, arrived)
    value = turned(TAU, image)
    term[...] = value
    low = low_rows(value)
    ghost = jnp.sum(got[pl.ds(6, NDEV, stride=8), :], axis=0, keepdims=True)
    ghost = ghost + pltpu.roll(ghost, 112, 1)
    ghost = jnp.where(lanes((1, 128)) < 16, ghost, 0.0)
    high = ghost.astype(BF).astype(F32)
    lows = pad_row(value)
    slopes = []
    for p in range(2):
        slopes += [slope[p : p + 1, 0:128], slope[p : p + 1, 128:256]]
    fill(message, slopes + [lows[0:1] + pltpu.roll(high, 96, 1), lows[1:2] + pltpu.roll(ghost - high, 96, 1),
                            jnp.zeros((2, 128), F32)])
    for k in range(2):
        part = jnp.dot(low, surface[k], preferred_element_type=F32)
        for p in range(2):
            for c in range(4):
                dest = (p * 2 + k) * 4 + c
                for half in range(2):
                    at = dest * 8 + 6 + half
                    lo = c * CH + half * 128
                    message[at : at + 1, :] = part[p : p + 1, lo : lo + 128]
    out[...] = message[...].reshape(NDEV, 8, 128).astype(BF)


def inner_second_kernel(idx, field, sizes, links, received, dipole, surface, first, energies, term, ghosts,
                        got, table, sums, rows_held, arrived, slopes):
    fetch_dipole(idx, links, dipole, rows_held, arrived)
    got[...] = received[...].astype(F32).reshape(NDEV * 8, 128)
    lane = lanes((NDEV, 128))
    pairs = jnp.where(lane < 112, got[pl.ds(4, NDEV, stride=8), :] + got[pl.ds(5, NDEV, stride=8), :], 0.0)
    ghosts[...] = pltpu.roll(pairs, 32, 1).T[0:16, :]
    for q in range(4):
        image = ghost_image(ghost_rows(ghosts, q))
        for p in range(2):
            extra = (4.0 * image[p][1] - 3.0 * image[p][0]) * (1.0 / (2.0 * STEP))
            for half in range(2):
                at = 8 * q + 2 * p + half
                total = got[at : at + 1, :] + extra[:, half * 128 : half * 128 + 128]
                row = p * 8 + q * 2 + half
                slopes[row : row + 1, :] = total.astype(BF).astype(F32)

    def slope_row(p, block128):
        return slopes[p * 8 + block128 : p * 8 + block128 + 1, :]

    image = apply_inner(idx, field, sizes, links, energies, got, dipole, surface, first[...], slope_row, table,
                        sums, rows_held, arrived)
    term[...] = turned(0.5 * TAU, image)


def fixed_block(block, i):
    return (block, 0)


def fixed_origin(i):
    return (0, 0)


def body(psi_outer, psi_inner, couplings, radial_parts, labels, surface, dipole_inner, energies, block_sizes,
         block_links, field):
    me = lax.axis_index("chan")
    rad = lax.axis_index("radial")
    idx = jnp.stack([me, rad, rad * NCHAN + me, jnp.zeros_like(me)]).astype(jnp.int32)
    everyone = ("radial", "chan")
    count = 64

    def chan_shift(x, s):
        return lax.ppermute(x, "chan", [(i, (i + s) % NCHAN) for i in range(NCHAN)])

    def core_swap(x):
        return lax.ppermute(x, "radial", [(i, i ^ 1) for i in range(count)])

    def edge_shift(x):
        pairs = []
        for r in range(count):
            for c in range(NCHAN):
                to, t = (r - 1, c + 1) if c % 2 == 0 else (r + 1, c - 1)
                if 0 <= to < count:
                    pairs.append((r * NCHAN + c, to * NCHAN + t))
        return lax.ppermute(x, everyone, pairs)

    def sector_shift(x):
        low = lax.ppermute(x, "radial", [(i, i + 1) for i in range(count - 1)])
        high = lax.ppermute(x, "radial", [(i + 1, i) for i in range(count - 1)])
        return low, high

    def exchange(x):
        return lax.all_to_all(x, everyone, 0, 0, tiled=True)

    tiles_first = Layout(major_to_minor=(0, 2, 1, 3))

    def flat(x):
        x = with_layout_constraint(x.reshape(CH, 2, 6, 128), tiles_first)
        return x.transpose(0, 2, 1, 3).reshape(CH * ROWS, 128)

    def unflat(x):
        x = with_layout_constraint(x.reshape(CH, 6, 2, 128).transpose(0, 2, 1, 3), tiles_first)
        return x.reshape(CH, 2, 768)

    u3 = flat(psi_outer)
    lab = labels.reshape(1, 1024)
    surf = jnp.swapaxes(surface, 1, 2)
    energy = energies.reshape(1, INNER)
    pack_shape = sds((PIECE + 1024, 128), BF)

    prepared = call(
        prepare_kernel,
        (sds((PIECE, 128), BF),) + (pack_shape,) * 3
        + (sds((72, CH), F32), sds((1024, 128), F32), sds((1024, CH), BF)),
        [SMEM, VMEM, VMEM, VMEM, VMEM], (idx, u3, couplings, lab, radial_parts), name="prepare")
    packs = prepared[0:4]
    edges, labcol, comb_own = prepared[4:]

    got = {s: chan_shift(packs[s], s) for s in (2, 1, 3)}
    mains = (packs[0], got[1], got[2], got[3])

    message1, now = call(
        inner_prepare_kernel, (sds((NDEV, 8, 128), BF), sds((2, INNER), F32)),
        [SMEM, SMEM, VMEM, VMEM, VMEM], (idx, block_sizes, psi_inner, edges, surf),
        [pltpu.VMEM((NDEV * 8, 128), F32), pltpu.VMEM((128, CH), F32)], name="inner_prepare")
    received1 = exchange(message1)
    edges, now = lax.optimization_barrier((edges, now))
    low, high = sector_shift(edges)
    mains, low, high = lax.optimization_barrier((mains, low, high))

    tails = [pl.BlockSpec((32, 128), functools.partial(fixed_block, (PART * m + CH) // 32)) for m in range(3)]
    whole = [pl.BlockSpec(x.shape, fixed_origin) for x in (comb_own, edges, lab, radial_parts)]
    slope, own = pl.pallas_call(
        boundary_kernel, grid=(1,), out_shape=(sds((2, CH), F32), sds((16, 1024), BF)),
        in_specs=[SMEM, SMEM] + tails * 4 + whole,
        out_specs=(pl.BlockSpec((2, CH), fixed_origin), pl.BlockSpec((16, 1024), fixed_origin)),
        scratch_shapes=[pltpu.VMEM((8, 1024), F32)], name="boundary",
        cost_estimate=pl.CostEstimate(flops=BOUNDARY_FLOPS, bytes_accessed=0, transcendentals=0),
        compiler_params=pltpu.CompilerParams(vmem_limit_bytes=60 << 20),
    )(idx, field, *[x for main in mains for x in (main,) * 3], comb_own, edges, lab, radial_parts)
    swapped = {s: core_swap(mains[s]) for s in (1, 3, 2)}
    beyond = edge_shift(own)

    inner_scratch = [
        pltpu.VMEM((NDEV * 8, 128), F32), pltpu.VMEM((2, 3, 64, 128), F32), pltpu.VMEM((2, INNER, 128), F32),
        pltpu.VMEM((INNER, 32 * BCAP), BF), pltpu.SemaphoreType.DMA((32,))]
    message2, inner_first = call(
        inner_first_kernel, (sds((NDEV, 8, 128), BF), sds((2, INNER), F32)),
        [SMEM] * 4 + [VMEM, ANY] + [VMEM] * 4,
        (idx, field, block_sizes, block_links, received1, dipole_inner, surf, now, energy, slope),
        inner_scratch + [pltpu.VMEM((NDEV * 8, 128), F32)], name="inner_first", flops=BESIDE_FLOPS)
    received2 = exchange(message2)
    comb_own, message2 = lax.optimization_barrier((comb_own, message2))

    partners = (comb_own, swapped[1], swapped[2], swapped[3])
    coupled = call(
        couple_kernel, (sds((CH, HALF + 128), BF),) * 4 + (sds((1024, 2 * HALF), BF),),
        [SMEM, SMEM] + [VMEM] * 13,
        (idx, field, *mains, beyond, *partners, low, high, labcol, radial_parts),
        [pltpu.VMEM((1024, 1024), BF), pltpu.VMEM((1024, 1024), BF), pltpu.VMEM((1024, 640), BF),
         pltpu.VMEM((1024, 1024), F32), pltpu.VMEM((1024, HALF), F32), pltpu.VMEM((512, 256), BF)], name="couple")
    pieces, pair2 = coupled[0:4], coupled[4]
    back = [pieces[0]] + [chan_shift(pieces[s], s) for s in (1, 2, 3)]
    pieces2 = call(
        couple_again_kernel, (sds((CH, HALF), BF),) * 4, [SMEM, SMEM] + [VMEM] * 10,
        (idx, field, *mains[1:], *partners, labcol, radial_parts, pair2),
        [pltpu.VMEM((1024, 1024), BF), pltpu.VMEM((1024, 2 * HALF), F32)], name="couple_again",
        flops=BESIDE_FLOPS)
    back2 = [pieces2[0]] + [chan_shift(pieces2[s], s) for s in (1, 2, 3)]


    received2, back = lax.optimization_barrier((received2, back))
    sums = jnp.sum(received2[:, 6:8, :].astype(F32), axis=0)
    later = [sums] + [lax.ppermute(sums, "radial", [(j, 0)]) for j in (1, 2, 3)]

    inner_second, ghosts = call(
        inner_second_kernel, (sds((2, INNER), F32), sds((16, CH), F32)), [SMEM] * 4 + [VMEM, ANY] + [VMEM] * 3,
        (idx, field, block_sizes, block_links, received2, dipole_inner, surf, inner_first, energy),
        inner_scratch + [pltpu.VMEM((16, 128), F32)], name="inner_second")

    back, ghosts = lax.optimization_barrier((back, ghosts))
    term_scratch = (
        [pltpu.VMEM((2, CH, 1024), F32)] + [pltpu.VMEM((2, CH, 1024), BF)] * 2
        + [pltpu.VMEM((2, CH, 1024), F32), pltpu.VMEM((512, 256), BF)])
    first3, sides = call(
        first_term_kernel, (sds((CH * ROWS, 128), F32), sds((2, CH, 128), F32)), [SMEM] + [VMEM] * 8,
        (idx, u3, low, high, *back, labcol), term_scratch + [pltpu.VMEM((2, CH, 256), F32)], name="first_term")
    second3 = call(
        second_term_kernel, sds((CH * ROWS, 128), F32), [SMEM] + [VMEM] * 7,
        (idx, first3, sides, *back2, labcol), term_scratch, name="second_term")

    tile = pl.BlockSpec((CH, 2, 128), lambda i: (0, 0, 0))
    outer_shape = sds((CH, 2, 768), F32)
    outer_first, outer_second = pl.pallas_call(
        fix_kernel, out_shape=(outer_shape, outer_shape), grid=(1,),
        in_specs=[SMEM, SMEM, tile, tile] + [VMEM] * 8, out_specs=(tile, tile),
        scratch_shapes=[pltpu.VMEM((8, 1024), F32)], input_output_aliases={2: 0, 3: 1}, name="fix",
        cost_estimate=pl.CostEstimate(flops=0, bytes_accessed=0, transcendentals=0),
        compiler_params=pltpu.CompilerParams(vmem_limit_bytes=60 << 20),
    )(idx, field, unflat(first3), unflat(second3), ghosts, *later, comb_own, lab, radial_parts)
    return outer_first, outer_second, inner_first, inner_second


def solution(mesh):
    in_specs = (
        P("chan", None, "radial"),
        P(None, ("radial", "chan")),
        P(None, None, "chan"),
        P(None, "radial"),
        P(),
        P(None, None, ("radial", "chan")),
        P(("radial", "chan"), None),
        P(("radial", "chan")),
        P(),
        P(),
        P(),
    )
    out_specs = (
        P("chan", None, "radial"),
        P("chan", None, "radial"),
        P(None, ("radial", "chan")),
        P(None, ("radial", "chan")),
    )
    return jax.shard_map(body, mesh=mesh, in_specs=in_specs, out_specs=out_specs, check_vma=False)
```

```python
import functools

import jax
import jax.numpy as jnp
from jax import lax
from jax.experimental import pallas as pl
from jax.experimental.pallas import tpu as pltpu
from jax.experimental.layout import Layout, with_layout_constraint
from jax.sharding import PartitionSpec as P

STEP = 0.2
INNER_RADIUS = 20.0
TAU = 0.025
LAP = 12.0 * STEP * STEP

CH = 256
ROWS = 12
NCHAN = 4
NDEV = 256
INNER = 96
HALF = 384
PART = CH + 32
PIECE = 3 * PART
BCAP = 768
BOUNDARY_FLOPS = 10**10
BESIDE_FLOPS = 3 * 10**10

BF = jnp.bfloat16
F32 = jnp.float32
VMEM = pl.BlockSpec(memory_space=pltpu.VMEM)
SMEM = pl.BlockSpec(memory_space=pltpu.SMEM)
ANY = pl.BlockSpec(memory_space=pl.ANY)


def sds(shape, dtype):
    return jax.ShapeDtypeStruct(shape, dtype)


def call(kernel, out_shape, specs, args, scratch=(), name=None, flops=0, limit=60):
    return pl.pallas_call(
        kernel,
        out_shape=out_shape,
        in_specs=specs,
        out_specs=jax.tree.map(lambda _: VMEM, out_shape),
        scratch_shapes=list(scratch),
        name=name,
        cost_estimate=pl.CostEstimate(flops=flops, bytes_accessed=0, transcendentals=0),
        compiler_params=pltpu.CompilerParams(vmem_limit_bytes=limit << 20),
    )(*args)


def lanes(shape):
    return lax.broadcasted_iota(jnp.int32, shape, len(shape) - 1)


def stencil(depth, width):
    gap = jnp.abs(lax.broadcasted_iota(jnp.int32, (depth, width), 0) - lanes((depth, width)) - 128)
    weight = jnp.where(gap == 0, -30.0, jnp.where(gap == 1, 16.0, jnp.where(gap == 2, -1.0, 0.0)))
    return weight.astype(BF)


def matmul(a, b):
    return jnp.dot(a, b, preferred_element_type=F32)


def inverse_square(start, width):
    pos = start + lanes((1, width))
    radius = INNER_RADIUS + (pos + 1).astype(F32) * STEP
    return 1.0 / (radius * radius)


def half_square(lab):
    return lab * (lab + 1.0) * 0.5


def parity(lab):
    return lab.astype(jnp.int32) & 1


def halo_tile(right, left):
    rows = jnp.concatenate([right, jnp.zeros((96, CH), F32), left], axis=0)
    return rows.T


def edge_rows(tile0, tile5):
    lane = lanes((CH, 128))
    return jnp.where(lane < 5, tile0, jnp.where((lane >= 12) & (lane < 16), pltpu.roll(tile5, 16, 1), 0.0))


def prepare_kernel(idx, u3, couplings, labels, radial_parts, m0, m1, m2, m3, edges, labcol, comb):
    me = idx[0]
    core = idx[1] & 1
    lab_rows = jnp.broadcast_to(labels[...].astype(F32), (128, 1024))
    labcol[...] = lab_rows.T
    mine = labels[:, pl.ds(pl.multiple_of(me * CH, CH), CH)].astype(F32)
    for part in range(4):
        rows = pl.ds(part * 256, 256)
        gap = jnp.abs(labcol[rows, 0:1] - mine)
        zero = couplings[0, rows, :].astype(F32)
        one = couplings[1, rows, :].astype(F32)
        value = jnp.where(gap == 1.0, zero, jnp.where((gap == 0.0) | (gap == 2.0), one, 0.0))
        comb[rows, :] = value.astype(BF)
    half = comb[pl.ds(pl.multiple_of(core * 512, 512), 512), :]
    for pack in (m1, m2, m3):
        pack[PIECE : PIECE + 512, :] = half[:, 0:128]
        pack[PIECE + 512 : PIECE + 1024, :] = half[:, 128:256]

    lane = lanes((CH, 128))
    picked = jnp.zeros((CH, 128), F32)
    for p in range(2):
        def tile(jb):
            return u3[pl.ds(2 * jb + p, CH, stride=ROWS), :]
        outer_edge = edge_rows(tile(0), tile(5))
        inner_edge = jnp.where(
            (lane == 16) | (lane == 17),
            pltpu.roll(tile(3), 16, 1),
            jnp.where((lane == 30) | (lane == 31), pltpu.roll(tile(2), 32, 1), 0.0),
        )
        both = outer_edge + inner_edge
        picked = picked + (both if p == 0 else pltpu.roll(both, 32, 1))
    edges[0:64, :] = picked.T[0:64, :]
    edges[64:66, :] = radial_parts[:, 0:256]
    edges[66:68, :] = radial_parts[:, 512:768]
    edges[68:72, :] = jnp.zeros((4, CH), F32)
    row8 = lax.broadcasted_iota(jnp.int32, (8, CH), 0)
    slab = jnp.where(row8 < 4, edges[0:8, :], pltpu.roll(edges[32:40, :], 4, 0))
    slab = jnp.concatenate([slab[:, 0:128], slab[:, 128:256]], axis=0).astype(BF)

    for s, main in enumerate((m0, m1, m2, m3)):
        t = (me + s) & 3
        p = t >> 1
        h = t & 1
        base = pl.multiple_of(p * 32, 32)
        inside = edges[pl.ds(base + 16, 16), :].astype(BF)
        own = edges[pl.ds(base, 16), :].astype(BF)
        tails = (inside[:, 0:128], inside[:, 128:256], slab)
        ends = (own[:, 0:128], own[:, 128:256], slab)
        for m in range(3):
            start = (3 * h + m) * 2 + p
            main[PART * m : PART * m + CH, :] = u3[pl.ds(start, CH, stride=ROWS), :].astype(BF)
            main[PART * m + CH : PART * m + CH + 16, :] = tails[m]
            main[PART * m + CH + 16 : PART * (m + 1), :] = ends[m]


def assemble(core, comb_own, own_half, other_half, comb):
    comb[:, 0:CH] = comb_own[...]
    ours = pl.ds(pl.multiple_of(core * 512, 512), 512)
    others = pl.ds(pl.multiple_of((1 - core) * 512, 512), 512)
    for s, (got, swapped) in enumerate(zip(own_half, other_half), 1):
        for half in range(2):
            at = s * CH + half * 128
            src = PIECE + 512 * half
            comb[ours, at : at + 128] = got[src : src + 512, :]
            comb[others, at : at + 128] = swapped[src : src + 512, :]


def couple_kernel(idx, field, m0, m1, m2, m3, comb_own, q1, q2, q3, labcol, radial_parts,
                  c0, c1, c2, c3, pair2, comb, pair, wide_u, both, laps, weights):
    me = idx[0]
    rad = idx[1]
    core = rad & 1
    p = me >> 1
    h = me & 1
    mains = (m0, m1, m2, m3)
    assemble(core, comb_own, (m1, m2, m3), (q1, q2, q3), comb)
    weights[...] = stencil(512, 256)
    for s in range(4):
        src = (me - s) & 3
        odd = parity(labcol[pl.ds(pl.multiple_of(src * CH, CH), CH), 0:1]).astype(F32)
        rows = slice(s * CH, (s + 1) * CH)
        main = mains[s]
        inside = jnp.concatenate([main[CH : CH + 16, :], main[PART + CH : PART + CH + 16, :]], axis=1).astype(F32)
        halo = halo_tile(jnp.where(h == 0, inside, 0.0), jnp.where(h == 0, 0.0, inside)).astype(BF)
        even16 = (1.0 - odd).astype(BF)
        odd16 = odd.astype(BF)
        wide_u[rows, 0:128] = halo
        wide_u[rows, 512:640] = halo
        for m in range(3):
            tile = main[PART * m : PART * m + CH, :]
            wide_u[rows, 128 * (m + 1) : 128 * (m + 2)] = tile
            pair[rows, 128 * m : 128 * m + 128] = tile * even16
            pair[rows, HALF + 128 * m : HALF + 128 * m + 128] = tile * odd16
    for n in range(3):
        cols = slice(n * 256, n * 256 + 256)
        both[:, cols] = matmul(comb[...], pair[:, cols])
    laps[:, 0:256] = matmul(wide_u[:, 0:512], weights[...])
    laps[:, 256:HALF] = matmul(wide_u[:, 256:640], weights[0:384, 0:128])
    inv = inverse_square(rad * 768 + h * HALF, HALF)
    scale = jnp.where(p == 1, TAU, -TAU)
    cols = pl.ds(pl.multiple_of(h * HALF, 128), HALF)
    row0 = radial_parts[0:1, cols] * field[0]
    row1 = radial_parts[1:2, cols]
    for target, out in enumerate((c0, c1, c2, c3)):
        t = (me + target) & 3
        s = (4 - target) % 4
        rows = pl.ds(pl.multiple_of(t * CH, CH), CH)
        spot = slice(s * CH, (s + 1) * CH)
        lab = labcol[rows, 0:1]
        even = parity(lab) == 0
        centrifugal = half_square(lab)
        for m in range(3):
            tile = slice(128 * m, 128 * m + 128)
            beside = slice(HALF + 128 * m, HALF + 128 * m + 128)
            a, b = both[rows, tile], both[rows, beside]
            coupled = row1[:, tile] * jnp.where(even, a, b) + row0[:, tile] * jnp.where(even, b, a)
            out[:, tile] = coupled.astype(BF)
            u = wide_u[spot, 128 * (m + 1) : 128 * (m + 2)].astype(F32)
            value = scale * (coupled + (-0.5 / LAP) * laps[spot, tile] + centrifugal * inv[:, tile] * u)
            pair2[spot, tile] = jnp.where(even, value, 0.0).astype(BF)
            pair2[spot, beside] = jnp.where(even, 0.0, value).astype(BF)


def couple_again_kernel(idx, field, m1, m2, m3, comb_own, q1, q2, q3, labcol, radial_parts, pair2, beyond, low, high,
                        c0, c1, c2, c3, comb, pair, both):
    me = idx[0]
    p = me >> 1
    h = me & 1
    assemble(idx[1] & 1, comb_own, (m1, m2, m3), (q1, q2, q3), comb)
    pair[:, 0 : 2 * HALF] = pair2[...]
    scale = jnp.where(p == 1, TAU, -TAU) * (-0.5 / LAP)
    row = lax.broadcasted_iota(jnp.int32, (16, CH), 0)
    for s in range(4):
        src = (me - s) & 3
        odd = parity(labcol[pl.ds(pl.multiple_of(src * CH, CH), CH), 0:1]) == 1
        rows = slice(s * CH, (s + 1) * CH)
        outside = beyond[:, pl.ds(pl.multiple_of(src * CH, CH), CH)].astype(F32)
        halo = halo_tile(outside, outside)
        pair[rows, 768:896] = jnp.where(odd, 0.0, halo).astype(BF)
        pair[rows, 896:1024] = jnp.where(odd, halo, 0.0).astype(BF)
        begin = jnp.where(row == 0, 16.0 * outside[15:16] - outside[14:15], jnp.where(row == 1, -outside[15:16], 0.0))
        end = jnp.where(row == 15, 16.0 * outside[0:1] - outside[1:2], jnp.where(row == 14, -outside[0:1], 0.0))
        edge = scale * halo_tile(jnp.where(h == 0, begin, 0.0), jnp.where(h == 0, 0.0, end))
        even_cols = pl.ds(pl.multiple_of(h * 256, 128), 128)
        odd_cols = pl.ds(pl.multiple_of(HALF + h * 256, 128), 128)
        pair[rows, even_cols] = (pair[rows, even_cols].astype(F32) + jnp.where(odd, 0.0, edge)).astype(BF)
        pair[rows, odd_cols] = (pair[rows, odd_cols].astype(F32) + jnp.where(odd, edge, 0.0)).astype(BF)
    for n in range(4):
        cols = slice(n * 256, n * 256 + 256)
        both[:, cols] = matmul(comb[...], pair[:, cols])
    cols = pl.ds(pl.multiple_of(h * HALF, 128), HALF)
    near = lanes((1, 128)) < 64
    row0 = jnp.concatenate(
        [radial_parts[0:1, cols], jnp.where(near, high[64:65, 0:128], low[66:67, 128:256])], axis=1) * field[0]
    row1 = jnp.concatenate(
        [radial_parts[1:2, cols], jnp.where(near, high[65:66, 0:128], low[67:68, 128:256])], axis=1)
    for target, out in enumerate((c0, c1, c2, c3)):
        t = (me + target) & 3
        rows = pl.ds(pl.multiple_of(t * CH, CH), CH)
        even = parity(labcol[rows, 0:1]) == 0
        for m in range(4):
            tile = slice(128 * m, 128 * m + 128)
            first, other = (768, 896) if m == 3 else (128 * m, HALF + 128 * m)
            a, b = both[rows, first : first + 128], both[rows, other : other + 128]
            coupled = row1[:, tile] * jnp.where(even, a, b) + row0[:, tile] * jnp.where(even, b, a)
            out[:, tile] = coupled.astype(BF)


def split(x):
    high = x.astype(BF)
    return high, (x - high.astype(F32)).astype(BF)


def store_split(upper, lower, p, cols, x):
    upper[p, :, cols], lower[p, :, cols] = split(x)


def stencil_window(upper, lower, weights, p, start, depth, width):
    part = slice(start, start + depth)
    w = weights[0:depth, 0:width]
    return matmul(upper[p, :, part], w) + matmul(lower[p, :, part], w)


def load_state(source3, halos, state, upper, lower, laps, weights):
    for p in range(2):
        for tile in range(8):
            cols = slice(128 * tile, 128 * tile + 128)
            x = halos[p] if tile in (0, 7) else source3[pl.ds(2 * (tile - 1) + p, CH, stride=ROWS), :]
            state[p, :, cols] = x
            store_split(upper, lower, p, cols, x)
    for p in range(2):
        for n in range(3):
            laps[p, :, 128 + 256 * n : 384 + 256 * n] = stencil_window(upper, lower, weights, p, 256 * n, 512, 256)


def first_term_kernel(idx, u3, low, high, c0, c1, c2, c3, labcol, first3, sides, state, upper, lower, laps, weights):
    me = idx[0]
    rad = idx[1]
    cs = (c0, c1, c2, c3)
    weights[...] = stencil(512, 256)
    halos = [halo_tile(high[p * 32 : p * 32 + 16, :], low[p * 32 : p * 32 + 16, :]) for p in range(2)]
    load_state(u3, halos, state, upper, lower, laps, weights)
    for p in range(2):
        w = weights[128:384, 0:128]
        laps[p, :, 0:128] = matmul(upper[p, :, 0:256], w) + matmul(lower[p, :, 0:256], w)
        laps[p, :, 896:1024] = stencil_window(upper, lower, weights, p, 768, 256, 128)
    lab = labcol[pl.ds(pl.multiple_of(me * CH, CH), CH), 0:1]
    centrifugal = half_square(lab)
    left = lanes((CH, 128)) >= 64
    for s in range(4):
        t = (me - s) & 3
        p = t >> 1
        h = t & 1
        scale = jnp.where(p == 1, TAU, -TAU)
        inv = inverse_square(rad * 768 + h * HALF, HALF)
        for m in range(3):
            tile = slice(128 * m, 128 * m + 128)
            cols = pl.ds(pl.multiple_of(h * HALF + 128 * (m + 1), 128), 128)
            value = scale * (cs[s][:, tile].astype(F32) + (-0.5 / LAP) * laps[p, :, cols]
                             + centrifugal * inv[:, tile] * state[p, :, cols])
            first3[pl.ds((3 * h + m) * 2 + 1 - p, CH, stride=ROWS), :] = value
    left_inv = inverse_square(rad * 768 - 128, 128)
    right_inv = inverse_square(rad * 768 + 768, 128)
    for p in range(2):
        scale = TAU if p == 1 else -TAU
        before = (-0.5 / LAP) * laps[p, :, 0:128] + centrifugal * left_inv * state[p, :, 0:128]
        after = (-0.5 / LAP) * laps[p, :, 896:1024] + centrifugal * right_inv * state[p, :, 896:1024]
        before = jnp.where(rad == 0, 0.0, before)
        after = jnp.where(rad == 63, 0.0, after)
        sides[1 - p] = scale * jnp.where(left, before, after)


def second_term_kernel(idx, first3, sides, c0, c1, c2, c3, labcol, second3, state, upper, lower, laps, weights, halos):
    me = idx[0]
    rad = idx[1]
    weights[...] = stencil(512, 256)
    left = lanes((CH, 128)) >= 64
    halos[...] = sides[...]
    for s, c in enumerate((c0, c1, c2, c3)):
        t = (me - s) & 3
        p = t >> 1
        h = t & 1
        scale = jnp.where(p == 1, TAU, -TAU)
        inside = jnp.where(h == 0, rad > 0, rad < 63)
        here = (left == (h == 0)) & inside
        halos[1 - p] = halos[1 - p] + jnp.where(here, scale * c[:, HALF : HALF + 128].astype(F32), 0.0)
    load_state(first3, (halos[0], halos[1]), state, upper, lower, laps, weights)
    centrifugal = half_square(labcol[pl.ds(pl.multiple_of(me * CH, CH), CH), 0:1])
    for s, c in enumerate((c0, c1, c2, c3)):
        t = (me - s) & 3
        p = 1 - (t >> 1)
        h = t & 1
        scale = jnp.where(p == 1, 0.5 * TAU, -0.5 * TAU)
        inv = inverse_square(rad * 768 + h * HALF, HALF)
        for m in range(3):
            tile = slice(128 * m, 128 * m + 128)
            cols = pl.ds(pl.multiple_of(h * HALF + 128 * (m + 1), 128), 128)
            value = scale * (c[:, tile].astype(F32) + (-0.5 / LAP) * laps[p, :, cols]
                             + centrifugal * inv[:, tile] * state[p, :, cols])
            second3[pl.ds((3 * h + m) * 2 + 1 - p, CH, stride=ROWS), :] = value


def split_couple(rows, comb, labels, me):
    odd = parity(labels[...]).astype(F32)
    from_even = jnp.dot((rows * (1.0 - odd)).astype(BF), comb[...], preferred_element_type=F32)
    from_odd = jnp.dot((rows * odd).astype(BF), comb[...], preferred_element_type=F32)
    mine_odd = parity(labels[:, pl.ds(pl.multiple_of(me * CH, CH), CH)]) == 1
    same = jnp.where(mine_odd, from_odd, from_even)
    other = jnp.where(mine_odd, from_even, from_odd)
    return same, other


def boundary_kernel(idx, field, a0, b0, t0, a1, b1, t1, a2, b2, t2, a3, b3, t3, comb, edges, labels, radial_parts, out, own, rows):
    me = idx[0]
    tails = ((a0, b0, t0), (a1, b1, t1), (a2, b2, t2), (a3, b3, t3))
    for s, (ends0, ends1, slab) in enumerate(tails):
        src = (me - s) & 3
        block = slab[0:16, :].astype(F32)
        at = pl.multiple_of(src * CH, CH)
        rows[:, pl.ds(at, 128)] = block[0:8]
        rows[:, pl.ds(at + 128, 128)] = block[8:16]
        own[:, pl.ds(at, 128)] = ends0[16:32, :]
        own[:, pl.ds(at + 128, 128)] = ends1[16:32, :]
    same, other = split_couple(rows[...], comb, labels, me)
    mine = labels[:, pl.ds(pl.multiple_of(me * CH, CH), CH)].astype(F32)
    image = []
    for p in range(2):
        w = [edges[p * 32 + j : p * 32 + j + 1, :] for j in range(5)]
        laps = (
            16.0 * w[1] - w[2] - 30.0 * w[0],
            16.0 * (w[0] + w[2]) - 30.0 * w[1] - w[3],
            16.0 * (w[1] + w[3]) - 30.0 * w[2] - w[0] - w[4],
        )
        terms = []
        for j in range(3):
            radius = INNER_RADIUS + (j + 1) * STEP
            r = p * 4 + j
            coupled = (field[0] * radial_parts[0:1, j : j + 1] * other[r : r + 1, :]
                       + radial_parts[1:2, j : j + 1] * same[r : r + 1, :])
            terms.append(-0.5 / LAP * laps[j] + half_square(mine) * (1.0 / (radius * radius)) * w[j] + coupled)
        image.append((4.0 * terms[1] - 3.0 * terms[0] - terms[2]) * (1.0 / (2.0 * STEP)))
    out[0:1, :] = TAU * image[1]
    out[1:2, :] = -TAU * image[0]


def ghost_image(g):
    image = [(-0.5 / LAP * (16.0 * g[p][1] - g[p][0]), 0.5 / LAP * g[p][1]) for p in range(2)]
    return [[TAU * image[1][j] for j in range(2)], [-TAU * image[0][j] for j in range(2)]]


def ghost_rows(ghosts, q):
    return [[ghosts[pl.ds((p * 2 + k) * 4 + q, 1), :] for k in range(2)] for p in range(2)]


def fix_kernel(idx, field, first_in, second_in, ghosts, b0, b1, b2, b3, comb, labels, radial_parts, first, second,
               rows):
    me = idx[0]
    on = jnp.where(idx[1] == 0, 1.0, 0.0)
    rows[...] = jnp.zeros((8, 1024), F32)
    for q in range(4):
        image = ghost_image(ghost_rows(ghosts, q))
        for p in range(2):
            for j in range(2):
                low = image[p][j].astype(BF).astype(F32)
                rows[p * 4 + j : p * 4 + j + 1, q * CH : (q + 1) * CH] = low
    same, other = split_couple(rows[...], comb, labels, me)
    mine = labels[:, pl.ds(pl.multiple_of(me * CH, CH), CH)].astype(F32)
    added = ghost_image(ghost_rows(ghosts, me))
    later = ((b0, b1), (b2, b3))
    images = []
    for p in range(2):
        g0, g1 = [jnp.concatenate([later[p][k][0:1, :], later[p][k][1:2, :]], axis=1) for k in range(2)]
        f0, f1 = added[p]
        laps = (16.0 * (f1 + g1) - 30.0 * f0 - g0, 16.0 * f0 - 30.0 * f1 - g1, 16.0 * f1 - f0, -f1)
        terms = [-0.5 / LAP * lap for lap in laps]
        for j in range(2):
            radius = INNER_RADIUS + (j + 1) * STEP
            r = p * 4 + j
            terms[j] = (terms[j] + half_square(mine) * (1.0 / (radius * radius)) * added[p][j]
                        + field[0] * radial_parts[0:1, j : j + 1] * other[r : r + 1, :]
                        + radial_parts[1:2, j : j + 1] * same[r : r + 1, :])
        images.append(terms)

    def columns(values):
        row = lax.broadcasted_iota(jnp.int32, (128, CH), 0)
        spread = jnp.zeros((128, CH), F32)
        for j, value in enumerate(values):
            spread = jnp.where(row == j, jnp.broadcast_to(value, (128, CH)), spread)
        return (spread * on).T

    for p in range(2):
        first[:, p, :] = first_in[:, p, :] + columns(added[p])
        sign = 0.5 * TAU if p == 0 else -0.5 * TAU
        second[:, p, :] = second_in[:, p, :] + columns([sign * term for term in images[1 - p]])


def active_row(idx, sizes):
    dev = idx[2]
    place = (dev & 7) * INNER + lanes((1, INNER))
    return (place < sizes[dev >> 3]).astype(F32)


def pad_row(row):
    return jnp.concatenate([row, jnp.zeros((row.shape[0], 128 - row.shape[1]), F32)], axis=1)


def low_rows(v):
    return jnp.concatenate([v, jnp.zeros((6, INNER), F32)], axis=0).astype(BF)


def fill(message, rows):
    tile = jnp.concatenate(rows, axis=0)
    message[...] = jnp.broadcast_to(tile[None], (NDEV, 8, 128)).reshape(NDEV * 8, 128)


def inner_prepare_kernel(idx, sizes, psi, edges, surface, out, now, message, table):
    v = psi[...] * active_row(idx, sizes)
    now[...] = v
    low = low_rows(v)
    slopes = []
    for p in range(2):
        w = [edges[p * 32 + j : p * 32 + j + 1, :] for j in range(3)]
        slope = (4.0 * w[1] - 3.0 * w[0] - w[2]) * (1.0 / (2.0 * STEP))
        slopes += [slope[:, 0:128], slope[:, 128:256]]
    lows = pad_row(v)
    fill(message, slopes + [lows[0:1], lows[1:2], jnp.zeros((2, 128), F32)])
    table[...] = jnp.zeros((128, CH), F32)
    for k in range(2):
        part = jnp.dot(low, surface[k], preferred_element_type=F32)
        for p in range(2):
            for q in range(4):
                at = (p * 2 + k) * 4 + q
                table[at : at + 1, :] = part[p : p + 1, q * CH : (q + 1) * CH]
    mine = table[...].T
    high = mine.astype(BF).astype(F32)
    message[pl.ds(6, NDEV, stride=8), :] = high + pltpu.roll(mine - high, 16, 1)
    out[...] = message[...].reshape(NDEV, 8, 128).astype(BF)


def dipole_copy(dipole, rows_held, arrived, b):
    cols = pl.ds(pl.multiple_of(b * BCAP, BCAP), BCAP)
    return pltpu.make_async_copy(dipole.at[:, cols], rows_held.at[:, cols], arrived.at[b])


def fetch_dipole(idx, links, dipole, rows_held, arrived):
    def step(b, _):
        @pl.when(links[idx[2] >> 3, b] != 0)
        def _():
            dipole_copy(dipole, rows_held, arrived, b).start()
        return 0

    lax.fori_loop(0, 32, step, 0)


def apply_inner(idx, field, sizes, links, energies, got, dipole, surface, v, slope_row, table, sums, rows_held,
                arrived):
    block = idx[2] >> 3
    lane = lanes((64, 128))
    for p in range(2):
        x = [got[pl.ds(4 + p + 8 * q, 64, stride=32), :] for q in range(4)]
        table[p, 0] = jnp.where(lane < 96, x[0], pltpu.roll(x[1], 96, 1))
        table[p, 1] = jnp.where(lane < 64, pltpu.roll(x[1], 96, 1), pltpu.roll(x[2], 64, 1))
        table[p, 2] = jnp.where(lane < 32, pltpu.roll(x[2], 64, 1), pltpu.roll(x[3], 32, 1))

    zero = jnp.zeros((INNER, 128), F32)
    for p in range(2):
        sums[p] = zero

    def step(b, _):
        @pl.when(links[block, b] != 0)
        def _():
            dipole_copy(dipole, rows_held, arrived, b).wait()
            totals = [zero, zero]
            for half in range(2):
                for m in range(3):
                    at = pl.multiple_of(b * BCAP + half * 384 + m * 128, 128)
                    tile = rows_held[:, pl.ds(at, 128)].astype(F32)
                    for p in range(2):
                        totals[p] = totals[p] + tile * table[p, m, pl.ds(2 * b + half, 1), :]
            for p in range(2):
                sums[p] = sums[p] + totals[p]
        return 0

    lax.fori_loop(0, 32, step, 0)
    rows = []
    for p in range(2):
        bloch = zero
        for block128 in range(8):
            tile = surface[1, :, block128 * 128 : block128 * 128 + 128].astype(F32)
            bloch = bloch + tile * slope_row(p, block128)
        total = field[0] * sums[p] + 0.5 * bloch
        total = jnp.concatenate([total, jnp.zeros((32, 128), F32)], axis=0)
        rows.append(jnp.sum(total.T, axis=0, keepdims=True)[:, 0:INNER])
    image = energies[...] * v + jnp.concatenate(rows, axis=0)
    return active_row(idx, sizes) * image


def turned(scale, image):
    return jnp.concatenate([scale * image[1:2], -scale * image[0:1]], axis=0)


def inner_first_kernel(idx, field, sizes, links, received, dipole, surface, now, energies, slope, out, term,
                       got, table, sums, rows_held, arrived, message):
    fetch_dipole(idx, links, dipole, rows_held, arrived)
    got[...] = received[...].astype(F32).reshape(NDEV * 8, 128)

    def slope_row(p, block128):
        src, half = block128 // 2, block128 % 2
        at = 8 * src + 2 * p + half
        return got[at : at + 1, :]

    image = apply_inner(idx, field, sizes, links, energies, got, dipole, surface, now[...], slope_row, table,
                        sums, rows_held, arrived)
    value = turned(TAU, image)
    term[...] = value
    low = low_rows(value)
    ghost = jnp.sum(got[pl.ds(6, NDEV, stride=8), :], axis=0, keepdims=True)
    ghost = ghost + pltpu.roll(ghost, 112, 1)
    ghost = jnp.where(lanes((1, 128)) < 16, ghost, 0.0)
    high = ghost.astype(BF).astype(F32)
    lows = pad_row(value)
    slopes = []
    for p in range(2):
        slopes += [slope[p : p + 1, 0:128], slope[p : p + 1, 128:256]]
    fill(message, slopes + [lows[0:1] + pltpu.roll(high, 96, 1), lows[1:2] + pltpu.roll(ghost - high, 96, 1),
                            jnp.zeros((2, 128), F32)])
    for k in range(2):
        part = jnp.dot(low, surface[k], preferred_element_type=F32)
        for p in range(2):
            for c in range(4):
                dest = (p * 2 + k) * 4 + c
                for half in range(2):
                    at = dest * 8 + 6 + half
                    lo = c * CH + half * 128
                    message[at : at + 1, :] = part[p : p + 1, lo : lo + 128]
    out[...] = message[...].reshape(NDEV, 8, 128).astype(BF)


def inner_second_kernel(idx, field, sizes, links, received, dipole, surface, first, energies, term, ghosts,
                        got, table, sums, rows_held, arrived, slopes):
    fetch_dipole(idx, links, dipole, rows_held, arrived)
    got[...] = received[...].astype(F32).reshape(NDEV * 8, 128)
    lane = lanes((NDEV, 128))
    pairs = jnp.where(lane < 112, got[pl.ds(4, NDEV, stride=8), :] + got[pl.ds(5, NDEV, stride=8), :], 0.0)
    ghosts[...] = pltpu.roll(pairs, 32, 1).T[0:16, :]
    for q in range(4):
        image = ghost_image(ghost_rows(ghosts, q))
        for p in range(2):
            extra = (4.0 * image[p][1] - 3.0 * image[p][0]) * (1.0 / (2.0 * STEP))
            for half in range(2):
                at = 8 * q + 2 * p + half
                total = got[at : at + 1, :] + extra[:, half * 128 : half * 128 + 128]
                row = p * 8 + q * 2 + half
                slopes[row : row + 1, :] = total.astype(BF).astype(F32)

    def slope_row(p, block128):
        return slopes[p * 8 + block128 : p * 8 + block128 + 1, :]

    image = apply_inner(idx, field, sizes, links, energies, got, dipole, surface, first[...], slope_row, table,
                        sums, rows_held, arrived)
    term[...] = turned(0.5 * TAU, image)


def fixed_block(block, i):
    return (block, 0)


def fixed_origin(i):
    return (0, 0)


def body(psi_outer, psi_inner, couplings, radial_parts, labels, surface, dipole_inner, energies, block_sizes,
         block_links, field):
    me = lax.axis_index("chan")
    rad = lax.axis_index("radial")
    idx = jnp.stack([me, rad, rad * NCHAN + me, jnp.zeros_like(me)]).astype(jnp.int32)
    everyone = ("radial", "chan")
    count = 64

    def chan_shift(x, s):
        return lax.ppermute(x, "chan", [(i, (i + s) % NCHAN) for i in range(NCHAN)])

    def core_swap(x):
        return lax.ppermute(x, "radial", [(i, i ^ 1) for i in range(count)])

    def edge_shift(x):
        pairs = []
        for r in range(count):
            for c in range(NCHAN):
                to, t = (r - 1, c + 1) if c % 2 == 0 else (r + 1, c - 1)
                if 0 <= to < count:
                    pairs.append((r * NCHAN + c, to * NCHAN + t))
        return lax.ppermute(x, everyone, pairs)

    def sector_shift(x):
        low = lax.ppermute(x, "radial", [(i, i + 1) for i in range(count - 1)])
        high = lax.ppermute(x, "radial", [(i + 1, i) for i in range(count - 1)])
        return low, high

    def exchange(x):
        return lax.all_to_all(x, everyone, 0, 0, tiled=True)

    tiles_first = Layout(major_to_minor=(0, 2, 1, 3))

    def flat(x):
        x = with_layout_constraint(x.reshape(CH, 2, 6, 128), tiles_first)
        return x.transpose(0, 2, 1, 3).reshape(CH * ROWS, 128)

    def unflat(x):
        x = with_layout_constraint(x.reshape(CH, 6, 2, 128).transpose(0, 2, 1, 3), tiles_first)
        return x.reshape(CH, 2, 768)

    u3 = flat(psi_outer)
    lab = labels.reshape(1, 1024)
    surf = jnp.swapaxes(surface, 1, 2)
    energy = energies.reshape(1, INNER)
    pack_shape = sds((PIECE + 1024, 128), BF)

    prepared = call(
        prepare_kernel,
        (sds((PIECE, 128), BF),) + (pack_shape,) * 3
        + (sds((72, CH), F32), sds((1024, 128), F32), sds((1024, CH), BF)),
        [SMEM, VMEM, VMEM, VMEM, VMEM], (idx, u3, couplings, lab, radial_parts), name="prepare")
    packs = prepared[0:4]
    edges, labcol, comb_own = prepared[4:]

    got = {s: chan_shift(packs[s], s) for s in (2, 1, 3)}
    mains = (packs[0], got[1], got[2], got[3])

    message1, now = call(
        inner_prepare_kernel, (sds((NDEV, 8, 128), BF), sds((2, INNER), F32)),
        [SMEM, SMEM, VMEM, VMEM, VMEM], (idx, block_sizes, psi_inner, edges, surf),
        [pltpu.VMEM((NDEV * 8, 128), F32), pltpu.VMEM((128, CH), F32)], name="inner_prepare")
    received1 = exchange(message1)
    edges, now = lax.optimization_barrier((edges, now))
    low, high = sector_shift(edges)

    tails = [pl.BlockSpec((32, 128), functools.partial(fixed_block, (PART * m + CH) // 32)) for m in range(3)]
    whole = [pl.BlockSpec(x.shape, fixed_origin) for x in (comb_own, edges, lab, radial_parts)]
    slope, own = pl.pallas_call(
        boundary_kernel, grid=(1,), out_shape=(sds((2, CH), F32), sds((16, 1024), BF)),
        in_specs=[SMEM, SMEM] + tails * 4 + whole,
        out_specs=(pl.BlockSpec((2, CH), fixed_origin), pl.BlockSpec((16, 1024), fixed_origin)),
        scratch_shapes=[pltpu.VMEM((8, 1024), F32)], name="boundary",
        cost_estimate=pl.CostEstimate(flops=BOUNDARY_FLOPS, bytes_accessed=0, transcendentals=0),
        compiler_params=pltpu.CompilerParams(vmem_limit_bytes=60 << 20),
    )(idx, field, *[x for main in mains for x in (main,) * 3], comb_own, edges, lab, radial_parts)
    swapped = {s: core_swap(mains[s]) for s in (1, 3, 2)}
    beyond = edge_shift(own)

    partners = (comb_own, swapped[1], swapped[2], swapped[3])
    coupled = call(
        couple_kernel, (sds((CH, HALF), BF),) * 4 + (sds((1024, 2 * HALF), BF),),
        [SMEM, SMEM] + [VMEM] * 10, (idx, field, *mains, *partners, labcol, radial_parts),
        [pltpu.VMEM((1024, 1024), BF), pltpu.VMEM((1024, 2 * HALF), BF), pltpu.VMEM((1024, 640), BF),
         pltpu.VMEM((1024, 2 * HALF), F32), pltpu.VMEM((1024, HALF), F32), pltpu.VMEM((512, 256), BF)],
        name="couple")
    pieces, pair2 = coupled[0:4], coupled[4]
    back = [pieces[0]] + [chan_shift(pieces[s], s) for s in (1, 2, 3)]
    received1, pair2, low, high = lax.optimization_barrier((received1, pair2, low, high))

    inner_scratch = [
        pltpu.VMEM((NDEV * 8, 128), F32), pltpu.VMEM((2, 3, 64, 128), F32), pltpu.VMEM((2, INNER, 128), F32),
        pltpu.VMEM((INNER, 32 * BCAP), BF), pltpu.SemaphoreType.DMA((32,))]
    message2, inner_first = call(
        inner_first_kernel, (sds((NDEV, 8, 128), BF), sds((2, INNER), F32)),
        [SMEM] * 4 + [VMEM, ANY] + [VMEM] * 4,
        (idx, field, block_sizes, block_links, received1, dipole_inner, surf, now, energy, slope),
        inner_scratch + [pltpu.VMEM((NDEV * 8, 128), F32)], name="inner_first", flops=BESIDE_FLOPS)
    received2 = exchange(message2)

    pair2, message2 = lax.optimization_barrier((pair2, message2))
    pieces2 = call(
        couple_again_kernel, (sds((CH, HALF + 128), BF),) * 4, [SMEM, SMEM] + [VMEM] * 13,
        (idx, field, *mains[1:], *partners, labcol, radial_parts, pair2, beyond, low, high),
        [pltpu.VMEM((1024, 1024), BF), pltpu.VMEM((1024, 1024), BF), pltpu.VMEM((1024, 1024), F32)],
        name="couple_again", flops=BESIDE_FLOPS)
    back2 = [pieces2[0]] + [chan_shift(pieces2[s], s) for s in (1, 2, 3)]

    received2, back = lax.optimization_barrier((received2, back))
    sums = jnp.sum(received2[:, 6:8, :].astype(F32), axis=0)
    later = [sums] + [lax.ppermute(sums, "radial", [(j, 0)]) for j in (1, 2, 3)]

    inner_second, ghosts = call(
        inner_second_kernel, (sds((2, INNER), F32), sds((16, CH), F32)), [SMEM] * 4 + [VMEM, ANY] + [VMEM] * 3,
        (idx, field, block_sizes, block_links, received2, dipole_inner, surf, inner_first, energy),
        inner_scratch + [pltpu.VMEM((16, 128), F32)], name="inner_second")

    back, ghosts = lax.optimization_barrier((back, ghosts))
    term_scratch = (
        [pltpu.VMEM((2, CH, 1024), F32)] + [pltpu.VMEM((2, CH, 1024), BF)] * 2
        + [pltpu.VMEM((2, CH, 1024), F32), pltpu.VMEM((512, 256), BF)])
    first3, sides = call(
        first_term_kernel, (sds((CH * ROWS, 128), F32), sds((2, CH, 128), F32)), [SMEM] + [VMEM] * 8,
        (idx, u3, low, high, *back, labcol), term_scratch, name="first_term")
    second3 = call(
        second_term_kernel, sds((CH * ROWS, 128), F32), [SMEM] + [VMEM] * 7,
        (idx, first3, sides, *back2, labcol), term_scratch + [pltpu.VMEM((2, CH, 128), F32)], name="second_term")

    tile = pl.BlockSpec((CH, 2, 128), lambda i: (0, 0, 0))
    outer_shape = sds((CH, 2, 768), F32)
    outer_first, outer_second = pl.pallas_call(
        fix_kernel, out_shape=(outer_shape, outer_shape), grid=(1,),
        in_specs=[SMEM, SMEM, tile, tile] + [VMEM] * 8, out_specs=(tile, tile),
        scratch_shapes=[pltpu.VMEM((8, 1024), F32)], input_output_aliases={2: 0, 3: 1}, name="fix",
        cost_estimate=pl.CostEstimate(flops=0, bytes_accessed=0, transcendentals=0),
        compiler_params=pltpu.CompilerParams(vmem_limit_bytes=60 << 20),
    )(idx, field, unflat(first3), unflat(second3), ghosts, *later, comb_own, lab, radial_parts)
    return outer_first, outer_second, inner_first, inner_second


def solution(mesh):
    in_specs = (
        P("chan", None, "radial"),
        P(None, ("radial", "chan")),
        P(None, None, "chan"),
        P(None, "radial"),
        P(),
        P(None, None, ("radial", "chan")),
        P(("radial", "chan"), None),
        P(("radial", "chan")),
        P(),
        P(),
        P(),
    )
    out_specs = (
        P("chan", None, "radial"),
        P("chan", None, "radial"),
        P(None, ("radial", "chan")),
        P(None, ("radial", "chan")),
    )
    return jax.shard_map(body, mesh=mesh, in_specs=in_specs, out_specs=out_specs, check_vma=False)
```
